32 devices in a mesh: ctx: 16 (over z, x, core), tp: 2 (over y).
Axes of the slice: x: 2, y: 2, z: 4, core: 2. Of those that a mesh axis runs over, the one named last changes fastest.
Arguments:
- q_in: float32 [8192, 2048], P('ctx', 'tp'), may hold values from -6 to 6
- k_in: float32 [8192, 2048], P('ctx', 'tp'), may hold values from -6 to 6
- v_in: float32 [8192, 2048], P('ctx', 'tp'), may hold values from -6 to 6
- short_taps: float32 [3, 3, 2048], P(None, None, 'tp'), may hold values from -3.5 to 3.5
- long_filter: float32 [8192, 2048], P('ctx', 'tp'), may hold values from -6 to 6
- skip_gain: float32 [2048], P('tp'), may hold values from 0.5 to 1.5
- conv_saved: float32 [8192, 2048], P('ctx', 'tp'), may hold values from -6 to 6
- grad_out: float32 [8192, 2048], P('ctx', 'tp'), may hold values from -6 to 6
Outputs:
- grad_q: float32 [8192, 2048], P('ctx', 'tp')
- grad_k: float32 [8192, 2048], P('ctx', 'tp')
- grad_v: float32 [8192, 2048], P('ctx', 'tp')
- grad_filter: float32 [2048, 8192], P(('ctx', 'tp'))
- grad_taps: float32 [3, 3, 2048], P(None, None, 'tp')
- grad_skip: float32 [2048], P('tp')
The draws below stay inside these ranges and needn't reach their ends.
All inputs are finite; a program needn't handle non-finite values.
Results may differ from the reference program's by a relative error of at most 0.00018.
Values sent between devices are 32-bit elements; how exact they have to be, the bound alone decides.
A program may use at most 128 MiB of HBM per device.

```python
import math
import jax
import jax.numpy as jnp
from jax import lax

C = 2048
SEQ = 8192


def block_scale(rng, shape, cuts, smallest, top_value):
    def one(dim, parts):
        steps = jax.random.uniform(jax.random.fold_in(jax.random.fold_in(rng, 6), dim), (parts,), jnp.float32, smallest / len(cuts), top_value / len(cuts))
        return jnp.repeat(jnp.exp(steps), shape[dim] // parts).reshape((-1,) + (1,) * (len(shape) - dim - 1))

    factor_of = one(*cuts[0])
    for cut in cuts[1:]:
        factor_of = factor_of * one(*cut)
    return factor_of


def noise(stream_key, extent, deviation, bound, shards=(), held_as=jnp.bfloat16):
    values = deviation * jax.random.normal(stream_key, extent, jnp.float32)
    if shards:
        values = values * block_scale(stream_key, extent, shards, -0.22, 0.18)
    return jnp.clip(values, -bound, bound).astype(held_as)


def setup_inputs(seed: int = 0) -> dict:
    keys = jax.random.split(jax.random.key(seed), 9)
    q_in = noise(keys[0], (SEQ, C), 1.0, 6.0, ((0, 16), (1, 2)), jnp.float32)
    k_in = noise(keys[1], (SEQ, C), 1.0, 6.0, ((0, 16), (1, 2)), jnp.float32)
    v_in = noise(keys[2], (SEQ, C), 1.0, 6.0, ((0, 16), (1, 2)), jnp.float32)
    short_taps = noise(keys[3], (3, 3, C), 3 ** -0.5, 3.5, ((2, 2),), jnp.float32)
    long_filter = noise(keys[4], (SEQ, C), 1.0, 6.0, ((0, 16), (1, 2)), jnp.float32)
    skip_gain = jnp.clip(0.5 + 1.0 * jax.random.uniform(keys[5], (C,), jnp.float32) ** block_scale(keys[5], (C,), ((0, 2),), -0.2, 0.2), 0.5, 1.5)
    conv_saved = noise(keys[6], (SEQ, C), 1.0, 6.0, ((0, 16), (1, 2)), jnp.float32)
    grad_out = noise(keys[7], (SEQ, C), 1.0, 6.0, ((0, 16), (1, 2)), jnp.float32)
    return {"q_in": q_in, "k_in": k_in, "v_in": v_in, "short_taps": short_taps, "long_filter": long_filter, "skip_gain": skip_gain, "conv_saved": conv_saved, "grad_out": grad_out}


def shorten(signal, weights):
    length = signal.shape[0]
    padded = jnp.pad(signal, ((2, 0), (0, 0)))
    return weights[0] * padded[2:] + weights[1] * padded[1:length + 1] + weights[2] * padded[:length]

def lengthen(grads, weights):
    length = grads.shape[0]
    padded = jnp.pad(grads, ((0, 2), (0, 0)))
    return weights[0] * padded[:length] + weights[1] * padded[1:length + 1] + weights[2] * padded[2:]

def tap_sums(grads, signal):
    length = signal.shape[0]
    padded = jnp.pad(signal, ((2, 0), (0, 0)))
    return jnp.stack([lax.optimization_barrier(jnp.sum(grads * padded[2 - offset:2 - offset + length], axis=0)) for offset in range(3)])

def correlate_block(pieces):
    filter_block, grad_block, zeta_block = pieces
    padded_length = 2 * SEQ
    spec_filter = jnp.fft.rfft(filter_block, n=padded_length, axis=0)
    spec_grad = jnp.fft.rfft(grad_block, n=padded_length, axis=0)
    spec_zeta = jnp.fft.rfft(zeta_block, n=padded_length, axis=0)
    corr_filter = jnp.fft.irfft(jnp.conj(spec_filter) * spec_grad, n=padded_length, axis=0)[:SEQ]
    corr_zeta = jnp.fft.irfft(jnp.conj(spec_zeta) * spec_grad, n=padded_length, axis=0)[:SEQ]
    return (corr_filter, corr_zeta)

def reference(q_in, k_in, v_in, short_taps, long_filter, skip_gain, conv_saved, grad_out):
    q_short = shorten(q_in, short_taps[0])
    k_short = shorten(k_in, short_taps[1])
    v_short = shorten(v_in, short_taps[2])
    product_kv = k_short * v_short
    grad_w = grad_out * q_short
    grad_qs = grad_out * conv_saved
    block_width = math.gcd(C, 256)
    block_count = C // block_width

    def to_blocks(array):
        return jnp.transpose(array.reshape(SEQ, block_count, block_width), (1, 0, 2))

    def from_blocks(array):
        return jnp.transpose(array, (1, 0, 2)).reshape(SEQ, C)
    corr_filter, corr_zeta = lax.map(correlate_block, (to_blocks(long_filter), to_blocks(grad_w), to_blocks(product_kv)))
    corr_filter = from_blocks(corr_filter)
    corr_zeta = from_blocks(corr_zeta)
    filter_scale = 1.0 / math.sqrt(SEQ)
    grad_z = skip_gain * grad_w + filter_scale * corr_filter
    grad_ks = grad_z * v_short
    grad_vs = grad_z * k_short
    grad_q = lengthen(grad_qs, short_taps[0])
    grad_k = lengthen(grad_ks, short_taps[1])
    grad_v = lengthen(grad_vs, short_taps[2])
    grad_taps = jnp.stack([tap_sums(grad_qs, q_in), tap_sums(grad_ks, k_in), tap_sums(grad_vs, v_in)])
    grad_skip = lax.optimization_barrier(jnp.sum(grad_w * product_kv, axis=0))
    grad_filter = jnp.transpose(filter_scale * corr_zeta)
    return (grad_q, grad_k, grad_v, grad_filter, grad_taps, grad_skip)
```

```python
import functools
import math

import jax
import jax.numpy as jnp
import numpy as np
from jax import lax
from jax.experimental import pallas as pl
from jax.experimental.pallas import tpu as pltpu
from jax.sharding import PartitionSpec as P

highest = lax.Precision.HIGHEST


def passed_along(value, axis, steps):
    count = lax.axis_size(axis)
    leading, last = (max(0, -steps), min(count, count - steps))
    return lax.ppermute(value, axis, [(source, source + steps) for source in range(leading, last)])


def phase_table(index_product, modulus, direction):
    reduced = jnp.mod(index_product, modulus).astype(jnp.float32)
    radians = direction * 2.0 * math.pi / modulus * reduced
    return (jnp.cos(radians), jnp.sin(radians))


def complex_mul(left_real, left_imag, right_real, right_imag):
    return (
        left_real * right_real - left_imag * right_imag,
        left_real * right_imag + left_imag * right_real,
    )


def matmul_complex(form, table_cos, table_sin, data_real, data_imag):
    real_out = jnp.einsum(form, table_cos, data_real, precision=highest) - jnp.einsum(
        form, table_sin, data_imag, precision=highest
    )
    imag_out = jnp.einsum(form, table_cos, data_imag, precision=highest) + jnp.einsum(
        form, table_sin, data_real, precision=highest
    )
    return (real_out, imag_out)


def channel_correlate(filter_real, filter_imag, grad_w, ctx_count):
    local_rows = filter_real.shape[0]
    slab_width = filter_real.shape[1]
    group_width = slab_width // ctx_count
    seq_total = local_rows * ctx_count
    arrived = (
        lax.all_to_all(filter_real, "ctx", split_axis=1, concat_axis=0, tiled=True),
        lax.all_to_all(filter_imag, "ctx", split_axis=1, concat_axis=0, tiled=True),
        lax.all_to_all(grad_w, "ctx", split_axis=1, concat_axis=0, tiled=True),
    )
    block_shape = (ctx_count, local_rows, group_width)
    whole_real = arrived[0].reshape(block_shape)
    whole_imag = arrived[1].reshape(block_shape)
    whole_grad = arrived[2].reshape(block_shape)
    spectral_index = lax.iota(jnp.int32, 2 * ctx_count)
    device_index = lax.iota(jnp.int32, ctx_count)
    position = lax.iota(jnp.int32, local_rows)
    outer_cos, outer_sin = phase_table(
        spectral_index[:, None] * device_index[None, :], 2 * ctx_count, -1.0
    )
    filter_pair = matmul_complex("qd,djc->qjc", outer_cos, outer_sin, whole_real, whole_imag)
    grad_pair = (
        jnp.einsum("qd,djc->qjc", outer_cos, whole_grad, precision=highest),
        jnp.einsum("qd,djc->qjc", outer_sin, whole_grad, precision=highest),
    )
    twist_cos, twist_sin = phase_table(
        spectral_index[:, None] * position[None, :], 2 * seq_total, -1.0
    )
    filter_pair = complex_mul(
        filter_pair[0], filter_pair[1], twist_cos[:, :, None], twist_sin[:, :, None]
    )
    grad_pair = complex_mul(
        grad_pair[0], grad_pair[1], twist_cos[:, :, None], twist_sin[:, :, None]
    )
    inner_cos, inner_sin = phase_table(position[:, None] * position[None, :], local_rows, -1.0)
    filter_spec = matmul_complex(
        "jb,qjc->qbc", inner_cos, inner_sin, filter_pair[0], filter_pair[1]
    )
    grad_spec = matmul_complex("jb,qjc->qbc", inner_cos, inner_sin, grad_pair[0], grad_pair[1])
    product_real = filter_spec[0] * grad_spec[0] + filter_spec[1] * grad_spec[1]
    product_imag = filter_spec[0] * grad_spec[1] - filter_spec[1] * grad_spec[0]
    back_cos, back_sin = phase_table(position[:, None] * position[None, :], local_rows, 1.0)
    summed = matmul_complex("jb,qbc->qjc", back_cos, back_sin, product_real, product_imag)
    untwist_cos, untwist_sin = phase_table(
        spectral_index[:, None] * position[None, :], 2 * seq_total, 1.0
    )
    summed = complex_mul(summed[0], summed[1], untwist_cos[:, :, None], untwist_sin[:, :, None])
    final_cos, final_sin = phase_table(
        device_index[:, None] * spectral_index[None, :], 2 * ctx_count, 1.0
    )
    result = matmul_complex("dq,qjc->djc", final_cos, final_sin, summed[0], summed[1])
    factor = 1.0 / (2.0 * seq_total)
    flat_shape = (seq_total, group_width)
    returned = (
        lax.all_to_all(
            (result[0] * factor).reshape(flat_shape), "ctx", split_axis=0, concat_axis=1, tiled=True
        ),
        lax.all_to_all(
            (result[1] * factor).reshape(flat_shape), "ctx", split_axis=0, concat_axis=1, tiled=True
        ),
    )
    return (returned[0], returned[1])


def on_device_general(q_in, k_in, v_in, short_taps, long_filter, skip_gain, conv_saved, grad_out):
    local_rows = q_in.shape[0]
    slab_width = q_in.shape[1]
    ctx_count = lax.axis_size("ctx")
    tp_count = lax.axis_size("tp")
    seq_total = local_rows * ctx_count
    filter_scale = 1.0 / math.sqrt(seq_total)
    inputs = jnp.stack([q_in, k_in, v_in])
    previous = passed_along(inputs[:, local_rows - 2 :], "ctx", 1)
    extended = jnp.concatenate([previous, inputs], axis=1)
    first_tap = short_taps[:, 0][:, None, :]
    second_tap = short_taps[:, 1][:, None, :]
    third_tap = short_taps[:, 2][:, None, :]
    shorted = (
        first_tap * extended[:, 2:]
        + second_tap * extended[:, 1 : local_rows + 1]
        + third_tap * extended[:, :local_rows]
    )
    q_short = shorted[0]
    k_short = shorted[1]
    v_short = shorted[2]
    product_kv = k_short * v_short
    grad_w = grad_out * q_short
    grad_qs = grad_out * conv_saved
    corr_real, corr_imag = channel_correlate(long_filter, product_kv, grad_w, ctx_count)
    grad_z = skip_gain * grad_w + filter_scale * corr_real
    grad_long = -filter_scale * corr_imag
    grad_ks = grad_z * v_short
    grad_vs = grad_z * k_short
    grad_stack = jnp.stack([grad_qs, grad_ks, grad_vs])
    following = passed_along(grad_stack[:, :2], "ctx", -1)
    ext_grads = jnp.concatenate([grad_stack, following], axis=1)
    grad_inputs = (
        first_tap * ext_grads[:, :local_rows]
        + second_tap * ext_grads[:, 1 : local_rows + 1]
        + third_tap * ext_grads[:, 2:]
    )
    short_part = jnp.stack(
        [
            jnp.sum(grad_stack * extended[:, 2 - offset : 2 - offset + local_rows], axis=1)
            for offset in range(3)
        ],
        axis=1,
    )
    skip_part = jnp.sum(grad_w * product_kv, axis=0)
    short_total, skip_total = lax.psum((short_part, skip_part), "ctx")
    group_width = slab_width // ctx_count
    repeat = ctx_count // tp_count
    flipped = jnp.transpose(grad_long).reshape(repeat, tp_count * group_width, local_rows)
    settled = lax.all_to_all(
        lax.all_to_all(flipped, "tp", split_axis=1, concat_axis=0, tiled=True),
        "ctx",
        split_axis=0,
        concat_axis=2,
        tiled=True,
    )
    grad_filter = settled.reshape(group_width, seq_total)
    return (grad_inputs[0], grad_inputs[1], grad_inputs[2], grad_filter, short_total, skip_total)


MESH = pl.DeviceIdType.MESH
LANES = 128
HALF = 64
N2 = 128
MIB = 1 << 20


def split_table(table):
    high = table.astype(jnp.bfloat16)
    low = (table - high.astype(np.float64)).astype(jnp.bfloat16)
    return np.concatenate([high, high, low], axis=-1)


def split_data(data):
    high = data.astype(jnp.bfloat16)
    low = (data - high.astype(jnp.float32)).astype(jnp.bfloat16)
    return jnp.concatenate([high, low, high], axis=0)


def dft_tables(seq_total):
    n1_used = seq_total // 2 // N2
    n1_total = 2 * n1_used
    length = n1_total * N2
    n1 = np.arange(n1_used)
    k1 = np.arange(n1_total)
    n2 = np.arange(N2)
    turns = (n1[None, None, :] * k1[None, :, None] * N2 + n2[:, None, None] * k1[None, :, None]) % length
    angle = 2.0 * np.pi / length * turns
    cos, sin = np.cos(angle), np.sin(angle)
    first = np.concatenate(
        [np.concatenate([cos, sin], axis=2), np.concatenate([-sin, cos], axis=2)], axis=1
    )
    factor = 1.0 / (length * math.sqrt(seq_total))
    cos_t, sin_t = np.swapaxes(cos, 1, 2) * factor, np.swapaxes(sin, 1, 2) * factor
    last = np.concatenate(
        [np.concatenate([cos_t, -sin_t], axis=2), np.concatenate([-sin_t, -cos_t], axis=2)], axis=1
    )
    inner = 2.0 * np.pi / N2 * ((n2[:, None] * n2[None, :]) % N2)
    c, s = np.cos(inner), np.sin(inner)
    second = np.block([[c, s], [-s, c]])
    back = np.block([[c, -s], [s, c]])
    odd = (np.arange(LANES) >= HALF)[None, :]
    turn_k2 = (2.0 * np.pi / N2 * n2)[:, None]
    turn_k1 = (2.0 * np.pi / length * k1)[:, None]
    phase_k2 = np.concatenate(
        [np.where(odd, np.cos(turn_k2), 1.0), np.where(odd, np.sin(turn_k2), 0.0)], axis=0
    ).astype(np.float32)
    phase_k1 = np.stack(
        [np.where(odd, np.cos(turn_k1), 1.0), np.where(odd, np.sin(turn_k1), 0.0)], axis=1
    ).astype(np.float32)
    return (
        split_table(first),
        split_table(second),
        split_table(back),
        split_table(last),
        phase_k2,
        phase_k1,
    )


def low_lanes(shape):
    return lax.broadcasted_iota(jnp.int32, shape, 1) < HALF


def swap(value):
    return pltpu.roll(value, HALF, 1)


def fft_kernel(
    f_ref, g_ref, k_ref, first_ref, second_ref, back_ref, last_ref, phase2_ref, phase1_ref,
    corr_ref, zeta_ref, yf_ref, yg_ref, z_ref,
):
    n1_used = f_ref.shape[0] // N2
    n1_total = 2 * n1_used
    tail = corr_ref.shape[0] - f_ref.shape[0]
    corr_ref[pl.ds(f_ref.shape[0], tail), :] = jnp.zeros((tail, LANES), jnp.float32)

    def forward(n2, carry):
        rows = pl.ds(n2, n1_used, stride=N2)
        xg = g_ref[rows, :]
        left = jnp.concatenate([f_ref[rows, :], k_ref[rows, :]], axis=0)
        right = jnp.concatenate([xg, jnp.zeros_like(xg)], axis=0)
        data = jnp.concatenate([left, right], axis=1)
        out = jnp.dot(first_ref[n2], split_data(data), preferred_element_type=jnp.float32)
        for part in range(2):
            into = pl.ds(n2 + part * N2, n1_total, stride=2 * N2)
            piece = out[part * n1_total : (part + 1) * n1_total]
            yf_ref[into, :] = piece[:, :LANES]
            yg_ref[into, :] = piece[:, LANES:]
        return carry

    lax.fori_loop(0, N2, forward, 0, unroll=4)

    low = low_lanes((N2, LANES))

    def product(k1):
        rows = pl.ds(pl.multiple_of(k1 * 2 * N2, 2 * N2), 2 * N2)
        data = jnp.concatenate([yf_ref[rows, :], yg_ref[rows, :]], axis=1)
        out = jnp.dot(second_ref[...], split_data(data), preferred_element_type=jnp.float32)
        fr, fi = out[:N2, :LANES], out[N2:, :LANES]
        gr, gi = out[:N2, LANES:], out[N2:, LANES:]
        sfr, sfi, sgr, sgi = swap(fr), swap(fi), swap(gr), swap(gi)
        er, ei = jnp.where(low, fr, sfr), jnp.where(low, fi, sfi)
        our, oui = jnp.where(low, sfr, fr), jnp.where(low, sfi, fi)
        ar, ai = phase2_ref[:N2, :], phase2_ref[N2:, :]
        both = phase1_ref[k1]
        br, bi = both[0:1], both[1:2]
        tr = ar * br - ai * bi
        ti = ar * bi + ai * br
        hr = tr * sgr - ti * sgi
        hi = tr * sgi + ti * sgr
        pr = er * gr + ei * gi + our * hr + oui * hi
        pi = er * gi - ei * gr + our * hi - oui * hr
        return jnp.concatenate([pr, pi], axis=0)

    def middle(pair, carry):
        k1 = pair * 2
        data = jnp.concatenate([product(k1), product(k1 + 1)], axis=1)
        out = jnp.dot(back_ref[...], split_data(data), preferred_element_type=jnp.float32)
        for part in range(2):
            for which in range(2):
                into = pl.ds(part * n1_total + k1 + which, N2, stride=2 * n1_total)
                z_ref[into, :] = out[
                    part * N2 : (part + 1) * N2, which * LANES : (which + 1) * LANES
                ]
        return carry

    lax.fori_loop(0, n1_total // 2, middle, 0)

    def inverse(n2, carry):
        rows = pl.ds(pl.multiple_of(n2 * 2 * n1_total, 2 * n1_total), 2 * n1_total)
        out = jnp.dot(last_ref[n2], split_data(z_ref[rows, :]), preferred_element_type=jnp.float32)
        into = pl.ds(n2, n1_used, stride=N2)
        corr_ref[into, :] = out[:n1_used]
        zeta_ref[into, :] = out[n1_used:]
        return carry

    lax.fori_loop(0, N2, inverse, 0, unroll=4)


def meet_all(ctx_count, tp_count, me_c, me_t):
    barrier = pltpu.get_barrier_semaphore()

    def greet(index, carry):
        c, t = index // tp_count, index % tp_count

        @pl.when(jnp.logical_or(c != me_c, t != me_t))
        def _():
            pl.semaphore_signal(barrier, inc=1, device_id={"ctx": c, "tp": t}, device_id_type=MESH)

        return carry

    lax.fori_loop(0, ctx_count * tp_count, greet, 0)
    pl.semaphore_wait(barrier, ctx_count * tp_count - 1)


def column(block):
    return pl.ds(pl.multiple_of(block * LANES, LANES), LANES)


def extend(ext_ref, array_ref, before, after, cols):
    rows = array_ref.shape[0]
    ext_ref[0:8, :] = before
    ext_ref[8 : 8 + rows, :] = array_ref[:, cols]
    ext_ref[8 + rows : 16 + rows, :] = after


def short_filter(ext_ref, taps_ref, branch, cols, count):
    return (
        taps_ref[branch, 0:1, cols] * ext_ref[8 : 8 + count, :]
        + taps_ref[branch, 1:2, cols] * ext_ref[7 : 7 + count, :]
        + taps_ref[branch, 2:3, cols] * ext_ref[6 : 6 + count, :]
    )


def long_gather(value_ref, taps_ref, branch, cols, count):
    return (
        taps_ref[branch, 0:1, cols] * value_ref[0:count, :]
        + taps_ref[branch, 1:2, cols] * value_ref[1 : 1 + count, :]
        + taps_ref[branch, 2:3, cols] * value_ref[2 : 2 + count, :]
    )


def tap_rows(value, ext_ref, count):
    return [
        jnp.sum(value * ext_ref[8 - o : 8 - o + count, :], axis=0, keepdims=True) for o in range(3)
    ]


def in_kernel(
    ctx_count, tp_count,
    q_ref, k_ref, v_ref, taps_ref, f_ref, saved_ref, out_grad_ref,
    rf_ref, rg_ref, rk_ref, grad_q_ref, tap_q_ref, before_ref, after_ref,
    pack_ref, ext_q, ext_k, ext_v, work, work2,
    halo_send, halo_recv, send_sem, recv_sem, self_sem,
):
    me_c, me_t = lax.axis_index("ctx"), lax.axis_index("tp")
    rows, width = q_ref.shape
    blocks = width // LANES
    half_rows = rows // 2
    first_owner = me_t * (ctx_count // tp_count)
    source_tp = me_c // (ctx_count // tp_count)
    received = (rf_ref, rg_ref, rk_ref)
    has_before, has_after = me_c > 0, me_c < ctx_count - 1
    low = low_lanes((half_rows, LANES))
    meet_all(ctx_count, tp_count, me_c, me_t)

    forward = [
        pltpu.make_async_remote_copy(
            src_ref=ref.at[pl.ds(rows - 8, 8)],
            dst_ref=before_ref.at[index],
            send_sem=halo_send.at[index],
            recv_sem=halo_recv.at[index],
            device_id={"ctx": jnp.minimum(me_c + 1, ctx_count - 1), "tp": me_t},
            device_id_type=MESH,
        )
        for index, ref in enumerate((q_ref, k_ref, v_ref))
    ]
    backward = [
        pltpu.make_async_remote_copy(
            src_ref=ref.at[pl.ds(0, 8)],
            dst_ref=after_ref.at[index],
            send_sem=halo_send.at[3 + index],
            recv_sem=halo_recv.at[3 + index],
            device_id={"ctx": jnp.maximum(me_c - 1, 0), "tp": me_t},
            device_id_type=MESH,
        )
        for index, ref in enumerate((q_ref, k_ref, v_ref, out_grad_ref, saved_ref))
    ]

    @pl.when(has_after)
    def _():
        for copy in forward:
            copy.start()

    @pl.when(has_before)
    def _():
        for copy in backward:
            copy.start()

    @pl.when(jnp.logical_not(has_before))
    def _():
        before_ref[...] = jnp.zeros_like(before_ref)

    @pl.when(jnp.logical_not(has_after))
    def _():
        after_ref[...] = jnp.zeros_like(after_ref)

    def block_copy(array, owner_c, owner_t, block):
        return pltpu.make_async_remote_copy(
            src_ref=pack_ref.at[array, block],
            dst_ref=received[array].at[pl.ds(pl.multiple_of(me_c * half_rows, half_rows), half_rows)],
            send_sem=send_sem.at[array, block],
            recv_sem=recv_sem.at[array, me_c],
            device_id={"ctx": owner_c, "tp": owner_t},
            device_id_type=MESH,
        )

    def self_copy(array, block):
        return pltpu.make_async_copy(
            pack_ref.at[array, block],
            received[array].at[pl.ds(pl.multiple_of(me_c * half_rows, half_rows), half_rows)],
            self_sem.at[array],
        )

    def is_self(owner_c, owner_t):
        return jnp.logical_and(owner_c == me_c, owner_t == me_t)

    def pack_and_send(array, column_block):
        even = work[pl.ds(0, half_rows, stride=2), :]
        odd = work[pl.ds(1, half_rows, stride=2), :]
        pack_ref[array, 2 * column_block] = jnp.where(low, even, swap(odd))
        pack_ref[array, 2 * column_block + 1] = jnp.where(low, swap(even), odd)
        owner_c = first_owner + column_block
        for owner_t in range(2):
            block = 2 * column_block + owner_t
            mine = is_self(owner_c, owner_t)

            @pl.when(mine)
            def _():
                self_copy(array, block).start()

            @pl.when(jnp.logical_not(mine))
            def _():
                block_copy(array, owner_c, owner_t, block).start()

    def send_filter(column_block, carry):
        work[0:rows, :] = f_ref[:, column(column_block)]
        pack_and_send(0, column_block)
        return carry

    lax.fori_loop(0, blocks, send_filter, 0)

    @pl.when(has_after)
    def _():
        for copy in forward:
            copy.wait_send()
        for copy in backward:
            copy.wait_recv()

    @pl.when(has_before)
    def _():
        for copy in forward:
            copy.wait_recv()
        for copy in backward:
            copy.wait_send()

    def send_grad(column_block, carry):
        cols = column(column_block)
        extend(ext_q, q_ref, before_ref[0, :, cols], after_ref[0, :, cols], cols)
        work[0:rows, :] = out_grad_ref[:, cols] * short_filter(ext_q, taps_ref, 0, cols, rows)
        pack_and_send(1, column_block)
        return carry

    lax.fori_loop(0, blocks, send_grad, 0)

    def send_product(column_block, carry):
        cols = column(column_block)
        extend(ext_k, k_ref, before_ref[1, :, cols], after_ref[1, :, cols], cols)
        extend(ext_v, v_ref, before_ref[2, :, cols], after_ref[2, :, cols], cols)
        work[0:rows, :] = short_filter(ext_k, taps_ref, 1, cols, rows) * short_filter(
            ext_v, taps_ref, 2, cols, rows
        )
        pack_and_send(2, column_block)
        return carry

    lax.fori_loop(0, blocks, send_product, 0)

    def query(column_block, carry):
        cols = column(column_block)
        extend(ext_q, q_ref, before_ref[0, :, cols], after_ref[0, :, cols], cols)
        here = out_grad_ref[:, cols] * saved_ref[:, cols]
        work2[0:rows, :] = here
        work2[rows : rows + 8, :] = after_ref[3, :, cols] * after_ref[4, :, cols]
        grad_q_ref[:, cols] = long_gather(work2, taps_ref, 0, cols, rows)
        sums = tap_rows(here, ext_q, rows)
        tap_q_ref[:, cols] = jnp.concatenate(sums + [jnp.zeros((5, LANES), jnp.float32)], axis=0)
        return carry

    lax.fori_loop(0, blocks, query, 0)

    for array in range(3):

        def settle(index, carry):
            owner_c, owner_t = first_owner + index // tp_count, index % tp_count
            mine = is_self(owner_c, owner_t)

            @pl.when(mine)
            def _():
                self_copy(array, index).wait()

            @pl.when(jnp.logical_not(mine))
            def _():
                block_copy(array, owner_c, owner_t, index).wait_send()

            @pl.when(jnp.logical_not(is_self(index, source_tp)))
            def _():
                pltpu.make_async_remote_copy(
                    src_ref=pack_ref.at[array, index],
                    dst_ref=received[array].at[
                        pl.ds(pl.multiple_of(index * half_rows, half_rows), half_rows)
                    ],
                    send_sem=send_sem.at[array, index],
                    recv_sem=recv_sem.at[array, index],
                    device_id={"ctx": index, "tp": source_tp},
                    device_id_type=MESH,
                ).wait_recv()

            return carry

        lax.fori_loop(0, ctx_count, settle, 0)


def out_kernel(
    ctx_count, tp_count,
    corr_ref, q_ref, k_ref, v_ref, out_grad_ref, taps_ref, skip_ref, tap_q_ref,
    before_ref, after_ref,
    grad_k_ref, grad_v_ref, total_ref,
    arrived, ext_q, ext_k, ext_v, grad_w, k_short, v_short, work, gk, gv, part, parts, summed,
    send_sem, recv_sem, self_sem, sum_send, sum_recv, spread_send, spread_recv,
):
    me_c, me_t = lax.axis_index("ctx"), lax.axis_index("tp")
    rows, width = q_ref.shape
    blocks = width // LANES
    half_rows = rows // 2
    more = half_rows + 8
    longer = rows + 8
    share = ctx_count // tp_count
    source_tp = me_c // share
    my_block = (me_c - source_tp * share) * tp_count + me_t
    meet_all(ctx_count, tp_count, me_c, me_t)

    def corr_rows(index):
        return corr_ref.at[pl.ds(pl.multiple_of(index * half_rows, half_rows), more)]

    def block_copy(index):
        return pltpu.make_async_remote_copy(
            src_ref=corr_rows(index),
            dst_ref=arrived.at[my_block],
            send_sem=send_sem.at[index],
            recv_sem=recv_sem.at[my_block],
            device_id={"ctx": index, "tp": source_tp},
            device_id_type=MESH,
        )

    def self_copy():
        return pltpu.make_async_copy(corr_rows(me_c), arrived.at[my_block], self_sem)

    def is_self(c, t):
        return jnp.logical_and(c == me_c, t == me_t)

    def launch(index, carry):
        mine = is_self(index, source_tp)

        @pl.when(mine)
        def _():
            self_copy().start()

        @pl.when(jnp.logical_not(mine))
        def _():
            block_copy(index).start()

        return carry

    lax.fori_loop(0, ctx_count, launch, 0)

    def prepare(column_block, carry):
        cols = column(column_block)
        extend(ext_q, q_ref, before_ref[0, :, cols], after_ref[0, :, cols], cols)
        extend(ext_k, k_ref, before_ref[1, :, cols], after_ref[1, :, cols], cols)
        extend(ext_v, v_ref, before_ref[2, :, cols], after_ref[2, :, cols], cols)
        q_short = short_filter(ext_q, taps_ref, 0, cols, longer)
        grad_w[0:rows, cols] = out_grad_ref[:, cols] * q_short[:rows]
        grad_w[rows:longer, cols] = after_ref[3, :, cols] * q_short[rows:]
        k_short[:, cols] = short_filter(ext_k, taps_ref, 1, cols, longer)
        v_short[:, cols] = short_filter(ext_v, taps_ref, 2, cols, longer)
        return carry

    lax.fori_loop(0, blocks, prepare, 0)

    def settle(index, carry):
        mine = is_self(index, source_tp)

        @pl.when(mine)
        def _():
            self_copy().wait()

        @pl.when(jnp.logical_not(mine))
        def _():
            block_copy(index).wait_send()

        owner_c, owner_t = me_t * share + index // tp_count, index % tp_count

        @pl.when(jnp.logical_not(is_self(owner_c, owner_t)))
        def _():
            pltpu.make_async_remote_copy(
                src_ref=corr_rows(index),
                dst_ref=arrived.at[index],
                send_sem=send_sem.at[index],
                recv_sem=recv_sem.at[index],
                device_id={"ctx": owner_c, "tp": owner_t},
                device_id_type=MESH,
            ).wait_recv()

        return carry

    lax.fori_loop(0, ctx_count, settle, 0)
    low = low_lanes((more, LANES))

    def finish(column_block, carry):
        cols = column(column_block)
        one, two = arrived[2 * column_block], arrived[2 * column_block + 1]
        work[pl.ds(0, more, stride=2), :] = jnp.where(low, one, swap(two))
        work[pl.ds(1, more, stride=2), :] = jnp.where(low, swap(one), two)
        extend(ext_k, k_ref, before_ref[1, :, cols], after_ref[1, :, cols], cols)
        extend(ext_v, v_ref, before_ref[2, :, cols], after_ref[2, :, cols], cols)
        weight, ks, vs = grad_w[:, cols], k_short[:, cols], v_short[:, cols]
        grad_z = skip_ref[0:1, cols] * weight + work[0:longer, :]
        gk[...] = grad_z * vs
        gv[...] = grad_z * ks
        grad_k_ref[:, cols] = long_gather(gk, taps_ref, 1, cols, rows)
        grad_v_ref[:, cols] = long_gather(gv, taps_ref, 2, cols, rows)
        sums = tap_rows(gk[0:rows, :], ext_k, rows) + tap_rows(gv[0:rows, :], ext_v, rows)
        skip = jnp.sum((weight * (ks * vs))[:rows], axis=0, keepdims=True)
        part[:, cols] = jnp.concatenate(
            [tap_q_ref[0:3, cols]] + sums + [skip, jnp.zeros((6, LANES), jnp.float32)], axis=0
        )
        return carry

    lax.fori_loop(0, blocks, finish, 0)

    def piece(ref, index):
        return ref.at[pl.ds(pl.multiple_of(index // blocks * 8, 8), 8), column(index % blocks)]

    def sum_copy(index, slot):
        return pltpu.make_async_remote_copy(
            src_ref=piece(part, index),
            dst_ref=parts.at[slot],
            send_sem=sum_send.at[index],
            recv_sem=sum_recv.at[slot],
            device_id={"ctx": index, "tp": me_t},
            device_id_type=MESH,
        )

    def spread_copy(index, slot):
        return pltpu.make_async_remote_copy(
            src_ref=summed,
            dst_ref=piece(total_ref, slot),
            send_sem=spread_send.at[index],
            recv_sem=spread_recv.at[slot],
            device_id={"ctx": index, "tp": me_t},
            device_id_type=MESH,
        )

    def others(action):
        def step(index, carry):
            @pl.when(index != me_c)
            def _():
                action(index)

            return carry

        lax.fori_loop(0, ctx_count, step, 0)

    others(lambda index: sum_copy(index, me_c).start())
    parts[me_c] = part[
        pl.ds(pl.multiple_of(me_c // blocks * 8, 8), 8), column(me_c % blocks)
    ]

    def sum_wait(index):
        sum_copy(index, me_c).wait_send()
        sum_copy(index, index).wait_recv()

    others(sum_wait)
    summed[...] = jnp.sum(parts[...], axis=0)
    others(lambda index: spread_copy(index, me_c).start())
    total_ref[pl.ds(pl.multiple_of(me_c // blocks * 8, 8), 8), column(me_c % blocks)] = summed[...]

    def spread_wait(index):
        spread_copy(index, me_c).wait_send()
        spread_copy(index, index).wait_recv()

    others(spread_wait)


def on_device(q_in, k_in, v_in, short_taps, long_filter, skip_gain, conv_saved, grad_out):
    rows, width = q_in.shape
    ctx_count, tp_count = lax.axis_size("ctx"), lax.axis_size("tp")
    group = width // ctx_count
    seq_total = rows * ctx_count
    fits = (
        tp_count == 2
        and group == HALF
        and ctx_count % 2 == 0
        and width == ctx_count // 2 * LANES
        and rows % 256 == 0
        and seq_total == 8192
    )
    if not fits:
        return on_device_general(
            q_in, k_in, v_in, short_taps, long_filter, skip_gain, conv_saved, grad_out
        )
    count = seq_total // 2
    f32 = jnp.float32
    vmem = pl.BlockSpec(memory_space=pltpu.VMEM)
    anywhere = pl.BlockSpec(memory_space=pl.ANY)
    shape = jax.ShapeDtypeStruct
    packed = shape((count, LANES), f32)
    dma = pltpu.SemaphoreType.DMA
    ext = pltpu.VMEM((rows + 16, LANES), f32)
    rf, rg, rk, grad_q, tap_q, before, after = pl.pallas_call(
        functools.partial(in_kernel, ctx_count, tp_count),
        out_shape=(
            packed, packed, packed,
            shape((rows, width), f32),
            shape((8, width), f32),
            shape((3, 8, width), f32),
            shape((5, 8, width), f32),
        ),
        in_specs=[vmem] * 7,
        out_specs=(anywhere, anywhere, anywhere, vmem, vmem, vmem, vmem),
        scratch_shapes=[
            pltpu.VMEM((3, ctx_count, rows // 2, LANES), f32),
            ext, ext, ext, ext, ext,
            dma((8,)), dma((8,)), dma((3, ctx_count)), dma((3, ctx_count)), dma((3,)),
        ],
        compiler_params=pltpu.CompilerParams(
            collective_id=0, has_side_effects=True, vmem_limit_bytes=56 * MIB
        ),
        name="send_in",
    )(q_in, k_in, v_in, short_taps, long_filter, conv_saved, grad_out)
    tables = [jnp.asarray(table) for table in dft_tables(seq_total)]
    corr, zeta = pl.pallas_call(
        fft_kernel,
        out_shape=(shape((count + 8, LANES), f32), packed),
        in_specs=[vmem] * 9,
        out_specs=(vmem, vmem),
        scratch_shapes=[
            pltpu.VMEM((2 * seq_total, LANES), f32),
            pltpu.VMEM((2 * seq_total, LANES), f32),
            pltpu.VMEM((2 * seq_total, LANES), f32),
        ],
        compiler_params=pltpu.CompilerParams(vmem_limit_bytes=60 * MIB),
        name="correlate",
    )(rf, rg, rk, *tables)
    longer = pltpu.VMEM((rows + 8, width), f32)
    grad_k, grad_v, total = pl.pallas_call(
        functools.partial(out_kernel, ctx_count, tp_count),
        out_shape=(shape((rows, width), f32), shape((rows, width), f32), shape((16, width), f32)),
        in_specs=[anywhere] + [vmem] * 9,
        out_specs=(vmem, vmem, vmem),
        scratch_shapes=[
            pltpu.VMEM((ctx_count, rows // 2 + 8, LANES), f32),
            ext, ext, ext, longer, longer, longer, ext,
            pltpu.VMEM((rows + 8, LANES), f32),
            pltpu.VMEM((rows + 8, LANES), f32),
            pltpu.VMEM((16, width), f32),
            pltpu.VMEM((ctx_count, 8, LANES), f32),
            pltpu.VMEM((8, LANES), f32),
            dma((ctx_count,)), dma((ctx_count,)), dma(()),
            dma((ctx_count,)), dma((ctx_count,)), dma((ctx_count,)), dma((ctx_count,)),
        ],
        compiler_params=pltpu.CompilerParams(
            collective_id=1, has_side_effects=True, vmem_limit_bytes=56 * MIB
        ),
        name="send_back",
    )(corr, q_in, k_in, v_in, grad_out, short_taps, skip_gain.reshape(1, width), tap_q, before, after)
    grad_filter = jnp.transpose(zeta.reshape(seq_total, HALF))
    return (grad_q, grad_k, grad_v, grad_filter, total[:9].reshape(3, 3, width), total[9])


def solution(mesh):
    placed = (
        P("ctx", "tp"),
        P("ctx", "tp"),
        P("ctx", "tp"),
        P(None, None, "tp"),
        P("ctx", "tp"),
        P("tp"),
        P("ctx", "tp"),
        P("ctx", "tp"),
    )
    return jax.shard_map(
        on_device,
        mesh=mesh,
        in_specs=placed,
        out_specs=(
            P("ctx", "tp"),
            P("ctx", "tp"),
            P("ctx", "tp"),
            P(("ctx", "tp"), None),
            P(None, None, "tp"),
            P("tp"),
        ),
        check_vma=False,
    )
```

```python
import functools
import math

import jax
import jax.numpy as jnp
import numpy as np
from jax import lax
from jax.experimental import pallas as pl
from jax.experimental.pallas import tpu as pltpu
from jax.sharding import PartitionSpec as P

highest = lax.Precision.HIGHEST


def passed_along(value, axis, steps):
    count = lax.axis_size(axis)
    leading, last = (max(0, -steps), min(count, count - steps))
    return lax.ppermute(value, axis, [(source, source + steps) for source in range(leading, last)])


def phase_table(index_product, modulus, direction):
    reduced = jnp.mod(index_product, modulus).astype(jnp.float32)
    radians = direction * 2.0 * math.pi / modulus * reduced
    return (jnp.cos(radians), jnp.sin(radians))


def complex_mul(left_real, left_imag, right_real, right_imag):
    return (
        left_real * right_real - left_imag * right_imag,
        left_real * right_imag + left_imag * right_real,
    )


def matmul_complex(form, table_cos, table_sin, data_real, data_imag):
    real_out = jnp.einsum(form, table_cos, data_real, precision=highest) - jnp.einsum(
        form, table_sin, data_imag, precision=highest
    )
    imag_out = jnp.einsum(form, table_cos, data_imag, precision=highest) + jnp.einsum(
        form, table_sin, data_real, precision=highest
    )
    return (real_out, imag_out)


def channel_correlate(filter_real, filter_imag, grad_w, ctx_count):
    local_rows = filter_real.shape[0]
    slab_width = filter_real.shape[1]
    group_width = slab_width // ctx_count
    seq_total = local_rows * ctx_count
    arrived = (
        lax.all_to_all(filter_real, "ctx", split_axis=1, concat_axis=0, tiled=True),
        lax.all_to_all(filter_imag, "ctx", split_axis=1, concat_axis=0, tiled=True),
        lax.all_to_all(grad_w, "ctx", split_axis=1, concat_axis=0, tiled=True),
    )
    block_shape = (ctx_count, local_rows, group_width)
    whole_real = arrived[0].reshape(block_shape)
    whole_imag = arrived[1].reshape(block_shape)
    whole_grad = arrived[2].reshape(block_shape)
    spectral_index = lax.iota(jnp.int32, 2 * ctx_count)
    device_index = lax.iota(jnp.int32, ctx_count)
    position = lax.iota(jnp.int32, local_rows)
    outer_cos, outer_sin = phase_table(
        spectral_index[:, None] * device_index[None, :], 2 * ctx_count, -1.0
    )
    filter_pair = matmul_complex("qd,djc->qjc", outer_cos, outer_sin, whole_real, whole_imag)
    grad_pair = (
        jnp.einsum("qd,djc->qjc", outer_cos, whole_grad, precision=highest),
        jnp.einsum("qd,djc->qjc", outer_sin, whole_grad, precision=highest),
    )
    twist_cos, twist_sin = phase_table(
        spectral_index[:, None] * position[None, :], 2 * seq_total, -1.0
    )
    filter_pair = complex_mul(
        filter_pair[0], filter_pair[1], twist_cos[:, :, None], twist_sin[:, :, None]
    )
    grad_pair = complex_mul(
        grad_pair[0], grad_pair[1], twist_cos[:, :, None], twist_sin[:, :, None]
    )
    inner_cos, inner_sin = phase_table(position[:, None] * position[None, :], local_rows, -1.0)
    filter_spec = matmul_complex(
        "jb,qjc->qbc", inner_cos, inner_sin, filter_pair[0], filter_pair[1]
    )
    grad_spec = matmul_complex("jb,qjc->qbc", inner_cos, inner_sin, grad_pair[0], grad_pair[1])
    product_real = filter_spec[0] * grad_spec[0] + filter_spec[1] * grad_spec[1]
    product_imag = filter_spec[0] * grad_spec[1] - filter_spec[1] * grad_spec[0]
    back_cos, back_sin = phase_table(position[:, None] * position[None, :], local_rows, 1.0)
    summed = matmul_complex("jb,qbc->qjc", back_cos, back_sin, product_real, product_imag)
    untwist_cos, untwist_sin = phase_table(
        spectral_index[:, None] * position[None, :], 2 * seq_total, 1.0
    )
    summed = complex_mul(summed[0], summed[1], untwist_cos[:, :, None], untwist_sin[:, :, None])
    final_cos, final_sin = phase_table(
        device_index[:, None] * spectral_index[None, :], 2 * ctx_count, 1.0
    )
    result = matmul_complex("dq,qjc->djc", final_cos, final_sin, summed[0], summed[1])
    factor = 1.0 / (2.0 * seq_total)
    flat_shape = (seq_total, group_width)
    returned = (
        lax.all_to_all(
            (result[0] * factor).reshape(flat_shape), "ctx", split_axis=0, concat_axis=1, tiled=True
        ),
        lax.all_to_all(
            (result[1] * factor).reshape(flat_shape), "ctx", split_axis=0, concat_axis=1, tiled=True
        ),
    )
    return (returned[0], returned[1])


def on_device_general(q_in, k_in, v_in, short_taps, long_filter, skip_gain, conv_saved, grad_out):
    local_rows = q_in.shape[0]
    slab_width = q_in.shape[1]
    ctx_count = lax.axis_size("ctx")
    tp_count = lax.axis_size("tp")
    seq_total = local_rows * ctx_count
    filter_scale = 1.0 / math.sqrt(seq_total)
    inputs = jnp.stack([q_in, k_in, v_in])
    previous = passed_along(inputs[:, local_rows - 2 :], "ctx", 1)
    extended = jnp.concatenate([previous, inputs], axis=1)
    first_tap = short_taps[:, 0][:, None, :]
    second_tap = short_taps[:, 1][:, None, :]
    third_tap = short_taps[:, 2][:, None, :]
    shorted = (
        first_tap * extended[:, 2:]
        + second_tap * extended[:, 1 : local_rows + 1]
        + third_tap * extended[:, :local_rows]
    )
    q_short = shorted[0]
    k_short = shorted[1]
    v_short = shorted[2]
    product_kv = k_short * v_short
    grad_w = grad_out * q_short
    grad_qs = grad_out * conv_saved
    corr_real, corr_imag = channel_correlate(long_filter, product_kv, grad_w, ctx_count)
    grad_z = skip_gain * grad_w + filter_scale * corr_real
    grad_long = -filter_scale * corr_imag
    grad_ks = grad_z * v_short
    grad_vs = grad_z * k_short
    grad_stack = jnp.stack([grad_qs, grad_ks, grad_vs])
    following = passed_along(grad_stack[:, :2], "ctx", -1)
    ext_grads = jnp.concatenate([grad_stack, following], axis=1)
    grad_inputs = (
        first_tap * ext_grads[:, :local_rows]
        + second_tap * ext_grads[:, 1 : local_rows + 1]
        + third_tap * ext_grads[:, 2:]
    )
    short_part = jnp.stack(
        [
            jnp.sum(grad_stack * extended[:, 2 - offset : 2 - offset + local_rows], axis=1)
            for offset in range(3)
        ],
        axis=1,
    )
    skip_part = jnp.sum(grad_w * product_kv, axis=0)
    short_total, skip_total = lax.psum((short_part, skip_part), "ctx")
    group_width = slab_width // ctx_count
    repeat = ctx_count // tp_count
    flipped = jnp.transpose(grad_long).reshape(repeat, tp_count * group_width, local_rows)
    settled = lax.all_to_all(
        lax.all_to_all(flipped, "tp", split_axis=1, concat_axis=0, tiled=True),
        "ctx",
        split_axis=0,
        concat_axis=2,
        tiled=True,
    )
    grad_filter = settled.reshape(group_width, seq_total)
    return (grad_inputs[0], grad_inputs[1], grad_inputs[2], grad_filter, short_total, skip_total)


MESH = pl.DeviceIdType.MESH
LANES = 128
HALF = 64
N2 = 128
MIB = 1 << 20


def split_table(table):
    high = table.astype(jnp.bfloat16)
    low = (table - high.astype(np.float64)).astype(jnp.bfloat16)
    return np.concatenate([high, high, low], axis=-1)


def split_data(data):
    high = data.astype(jnp.bfloat16)
    low = (data - high.astype(jnp.float32)).astype(jnp.bfloat16)
    return jnp.concatenate([high, low, high], axis=0)


def dft_tables(seq_total):
    n1_used = seq_total // 2 // N2
    n1_total = 2 * n1_used
    length = n1_total * N2
    n1 = np.arange(n1_used)
    k1 = np.arange(n1_total)
    n2 = np.arange(N2)
    turns = (n1[None, None, :] * k1[None, :, None] * N2 + n2[:, None, None] * k1[None, :, None]) % length
    angle = 2.0 * np.pi / length * turns
    cos, sin = np.cos(angle), np.sin(angle)
    first = np.concatenate(
        [np.concatenate([cos, sin], axis=2), np.concatenate([-sin, cos], axis=2)], axis=1
    )
    factor = 1.0 / (length * math.sqrt(seq_total))
    cos_t, sin_t = np.swapaxes(cos, 1, 2) * factor, np.swapaxes(sin, 1, 2) * factor
    last = np.concatenate(
        [np.concatenate([cos_t, -sin_t], axis=2), np.concatenate([-sin_t, -cos_t], axis=2)], axis=1
    )
    inner = 2.0 * np.pi / N2 * ((n2[:, None] * n2[None, :]) % N2)
    c, s = np.cos(inner), np.sin(inner)
    second = np.block([[c, s], [-s, c]])
    back = np.block([[c, -s], [s, c]])
    odd = (np.arange(LANES) >= HALF)[None, :]
    turn_k2 = (2.0 * np.pi / N2 * n2)[:, None]
    turn_k1 = (2.0 * np.pi / length * k1)[:, None]
    phase_k2 = np.concatenate(
        [np.where(odd, np.cos(turn_k2), 1.0), np.where(odd, np.sin(turn_k2), 0.0)], axis=0
    ).astype(np.float32)
    phase_k1 = np.stack(
        [np.where(odd, np.cos(turn_k1), 1.0), np.where(odd, np.sin(turn_k1), 0.0)], axis=1
    ).astype(np.float32)
    return (
        split_table(first),
        split_table(second),
        split_table(back),
        split_table(last),
        phase_k2,
        phase_k1,
    )


def low_lanes(shape):
    return lax.broadcasted_iota(jnp.int32, shape, 1) < HALF


def swap(value):
    return pltpu.roll(value, HALF, 1)


def fft_kernel(
    f_ref, g_ref, k_ref, first_ref, second_ref, back_ref, last_ref, phase2_ref, phase1_ref,
    corr_ref, zeta_ref, yf_ref, yg_ref, z_ref,
):
    n1_used = f_ref.shape[0] // N2
    n1_total = 2 * n1_used
    tail = corr_ref.shape[0] - f_ref.shape[0]
    corr_ref[pl.ds(f_ref.shape[0], tail), :] = jnp.zeros((tail, LANES), jnp.float32)

    def forward(n2, carry):
        rows = pl.ds(n2, n1_used, stride=N2)
        xg = g_ref[rows, :]
        left = jnp.concatenate([f_ref[rows, :], k_ref[rows, :]], axis=0)
        right = jnp.concatenate([xg, jnp.zeros_like(xg)], axis=0)
        data = jnp.concatenate([left, right], axis=1)
        out = jnp.dot(first_ref[n2], split_data(data), preferred_element_type=jnp.float32)
        for part in range(2):
            into = pl.ds(n2 + part * N2, n1_total, stride=2 * N2)
            piece = out[part * n1_total : (part + 1) * n1_total]
            yf_ref[into, :] = piece[:, :LANES]
            yg_ref[into, :] = piece[:, LANES:]
        return carry

    lax.fori_loop(0, N2, forward, 0, unroll=4)

    low = low_lanes((N2, LANES))

    def product(k1):
        rows = pl.ds(pl.multiple_of(k1 * 2 * N2, 2 * N2), 2 * N2)
        data = jnp.concatenate([yf_ref[rows, :], yg_ref[rows, :]], axis=1)
        out = jnp.dot(second_ref[...], split_data(data), preferred_element_type=jnp.float32)
        fr, fi = out[:N2, :LANES], out[N2:, :LANES]
        gr, gi = out[:N2, LANES:], out[N2:, LANES:]
        sfr, sfi, sgr, sgi = swap(fr), swap(fi), swap(gr), swap(gi)
        er, ei = jnp.where(low, fr, sfr), jnp.where(low, fi, sfi)
        our, oui = jnp.where(low, sfr, fr), jnp.where(low, sfi, fi)
        ar, ai = phase2_ref[:N2, :], phase2_ref[N2:, :]
        both = phase1_ref[k1]
        br, bi = both[0:1], both[1:2]
        tr = ar * br - ai * bi
        ti = ar * bi + ai * br
        hr = tr * sgr - ti * sgi
        hi = tr * sgi + ti * sgr
        pr = er * gr + ei * gi + our * hr + oui * hi
        pi = er * gi - ei * gr + our * hi - oui * hr
        return jnp.concatenate([pr, pi], axis=0)

    def middle(pair, carry):
        k1 = pair * 2
        data = jnp.concatenate([product(k1), product(k1 + 1)], axis=1)
        out = jnp.dot(back_ref[...], split_data(data), preferred_element_type=jnp.float32)
        for part in range(2):
            for which in range(2):
                into = pl.ds(part * n1_total + k1 + which, N2, stride=2 * n1_total)
                z_ref[into, :] = out[
                    part * N2 : (part + 1) * N2, which * LANES : (which + 1) * LANES
                ]
        return carry

    lax.fori_loop(0, n1_total // 2, middle, 0, unroll=2)

    def inverse(n2, carry):
        rows = pl.ds(pl.multiple_of(n2 * 2 * n1_total, 2 * n1_total), 2 * n1_total)
        out = jnp.dot(last_ref[n2], split_data(z_ref[rows, :]), preferred_element_type=jnp.float32)
        into = pl.ds(n2, n1_used, stride=N2)
        corr_ref[into, :] = out[:n1_used]
        zeta_ref[into, :] = out[n1_used:]
        return carry

    lax.fori_loop(0, N2, inverse, 0, unroll=4)


def meet_all(ctx_count, tp_count, me_c, me_t):
    barrier = pltpu.get_barrier_semaphore()

    def greet(index, carry):
        c, t = index // tp_count, index % tp_count

        @pl.when(jnp.logical_or(c != me_c, t != me_t))
        def _():
            pl.semaphore_signal(barrier, inc=1, device_id={"ctx": c, "tp": t}, device_id_type=MESH)

        return carry

    lax.fori_loop(0, ctx_count * tp_count, greet, 0)
    pl.semaphore_wait(barrier, ctx_count * tp_count - 1)


def column(block):
    return pl.ds(pl.multiple_of(block * LANES, LANES), LANES)


def extend(ext_ref, array_ref, before, after, cols):
    rows = array_ref.shape[0]
    ext_ref[0:8, :] = before
    ext_ref[8 : 8 + rows, :] = array_ref[:, cols]
    ext_ref[8 + rows : 16 + rows, :] = after


def short_filter(ext_ref, taps_ref, branch, cols, count):
    return (
        taps_ref[branch, 0:1, cols] * ext_ref[8 : 8 + count, :]
        + taps_ref[branch, 1:2, cols] * ext_ref[7 : 7 + count, :]
        + taps_ref[branch, 2:3, cols] * ext_ref[6 : 6 + count, :]
    )


def long_gather(value_ref, taps_ref, branch, cols, count):
    return (
        taps_ref[branch, 0:1, cols] * value_ref[0:count, :]
        + taps_ref[branch, 1:2, cols] * value_ref[1 : 1 + count, :]
        + taps_ref[branch, 2:3, cols] * value_ref[2 : 2 + count, :]
    )


def tap_rows(value, ext_ref, count):
    return [
        jnp.sum(value * ext_ref[8 - o : 8 - o + count, :], axis=0, keepdims=True) for o in range(3)
    ]


def in_kernel(
    ctx_count, tp_count,
    q_ref, k_ref, v_ref, taps_ref, f_ref, saved_ref, out_grad_ref,
    rf_ref, rg_ref, rk_ref, grad_q_ref, tap_q_ref, before_ref, after_ref,
    pack_ref, relay_ref, ext_q, ext_k, ext_v, work, work2,
    halo_send, halo_recv, send_sem, recv_sem, self_sem, relay_send, relay_recv,
):
    me_c, me_t = lax.axis_index("ctx"), lax.axis_index("tp")
    rows, width = q_ref.shape
    blocks = width // LANES
    half_rows = rows // 2
    first_owner = me_t * (ctx_count // tp_count)
    other_owner = (1 - me_t) * (ctx_count // tp_count)
    received = (rf_ref, rg_ref, rk_ref)
    has_before, has_after = me_c > 0, me_c < ctx_count - 1
    low = low_lanes((half_rows, LANES))
    meet_all(ctx_count, tp_count, me_c, me_t)

    forward = [
        pltpu.make_async_remote_copy(
            src_ref=ref.at[pl.ds(rows - 8, 8)],
            dst_ref=before_ref.at[index],
            send_sem=halo_send.at[index],
            recv_sem=halo_recv.at[index],
            device_id={"ctx": jnp.minimum(me_c + 1, ctx_count - 1), "tp": me_t},
            device_id_type=MESH,
        )
        for index, ref in enumerate((q_ref, k_ref, v_ref))
    ]
    backward = [
        pltpu.make_async_remote_copy(
            src_ref=ref.at[pl.ds(0, 8)],
            dst_ref=after_ref.at[index],
            send_sem=halo_send.at[3 + index],
            recv_sem=halo_recv.at[3 + index],
            device_id={"ctx": jnp.maximum(me_c - 1, 0), "tp": me_t},
            device_id_type=MESH,
        )
        for index, ref in enumerate((q_ref, k_ref, v_ref, out_grad_ref, saved_ref))
    ]

    @pl.when(has_after)
    def _():
        for copy in forward:
            copy.start()

    @pl.when(has_before)
    def _():
        for copy in backward:
            copy.start()

    @pl.when(jnp.logical_not(has_before))
    def _():
        before_ref[...] = jnp.zeros_like(before_ref)

    @pl.when(jnp.logical_not(has_after))
    def _():
        after_ref[...] = jnp.zeros_like(after_ref)

    def landing(array, source):
        return received[array].at[pl.ds(pl.multiple_of(source * half_rows, half_rows), half_rows)]

    def plane_copy(array, source_ref, owner, source):
        return pltpu.make_async_remote_copy(
            src_ref=source_ref,
            dst_ref=landing(array, source),
            send_sem=send_sem.at[array, owner],
            recv_sem=recv_sem.at[array, source],
            device_id={"ctx": owner, "tp": me_t},
            device_id_type=MESH,
        )

    def self_copy(array, source_ref):
        return pltpu.make_async_copy(source_ref, landing(array, me_c), self_sem.at[array])

    def send_in_plane(array, source_ref, owner):
        @pl.when(owner == me_c)
        def _():
            self_copy(array, source_ref).start()

        @pl.when(owner != me_c)
        def _():
            plane_copy(array, source_ref, owner, me_c).start()

    def relay_copy(array, column_block):
        return pltpu.make_async_remote_copy(
            src_ref=pack_ref.at[array, 1 - me_t, column_block],
            dst_ref=relay_ref.at[array, column_block],
            send_sem=relay_send.at[array, column_block],
            recv_sem=relay_recv.at[array, column_block],
            device_id={"ctx": me_c, "tp": 1 - me_t},
            device_id_type=MESH,
        )

    def pack_and_send(array, column_block):
        even = work[pl.ds(0, half_rows, stride=2), :]
        odd = work[pl.ds(1, half_rows, stride=2), :]
        pack_ref[array, 0, column_block] = jnp.where(low, even, swap(odd))
        pack_ref[array, 1, column_block] = jnp.where(low, swap(even), odd)
        relay_copy(array, column_block).start()
        send_in_plane(array, pack_ref.at[array, me_t, column_block], first_owner + column_block)

    def hand_on(array, column_block):
        relay_copy(array, column_block).wait_recv()
        send_in_plane(array, relay_ref.at[array, column_block], other_owner + column_block)

    def send_filter(column_block, carry):
        work[0:rows, :] = f_ref[:, column(column_block)]
        pack_and_send(0, column_block)
        return carry

    lax.fori_loop(0, blocks, send_filter, 0)

    @pl.when(has_after)
    def _():
        for copy in forward:
            copy.wait_send()
        for copy in backward:
            copy.wait_recv()

    @pl.when(has_before)
    def _():
        for copy in forward:
            copy.wait_recv()
        for copy in backward:
            copy.wait_send()

    def send_grad(column_block, carry):
        cols = column(column_block)
        extend(ext_q, q_ref, before_ref[0, :, cols], after_ref[0, :, cols], cols)
        work[0:rows, :] = out_grad_ref[:, cols] * short_filter(ext_q, taps_ref, 0, cols, rows)
        pack_and_send(1, column_block)
        hand_on(0, column_block)
        return carry

    lax.fori_loop(0, blocks, send_grad, 0)

    def send_product(column_block, carry):
        cols = column(column_block)
        extend(ext_k, k_ref, before_ref[1, :, cols], after_ref[1, :, cols], cols)
        extend(ext_v, v_ref, before_ref[2, :, cols], after_ref[2, :, cols], cols)
        work[0:rows, :] = short_filter(ext_k, taps_ref, 1, cols, rows) * short_filter(
            ext_v, taps_ref, 2, cols, rows
        )
        pack_and_send(2, column_block)
        hand_on(1, column_block)
        return carry

    lax.fori_loop(0, blocks, send_product, 0)

    def query(column_block, carry):
        cols = column(column_block)
        extend(ext_q, q_ref, before_ref[0, :, cols], after_ref[0, :, cols], cols)
        here = out_grad_ref[:, cols] * saved_ref[:, cols]
        work2[0:rows, :] = here
        work2[rows : rows + 8, :] = after_ref[3, :, cols] * after_ref[4, :, cols]
        grad_q_ref[:, cols] = long_gather(work2, taps_ref, 0, cols, rows)
        sums = tap_rows(here, ext_q, rows)
        tap_q_ref[:, cols] = jnp.concatenate(sums + [jnp.zeros((5, LANES), jnp.float32)], axis=0)
        return carry

    lax.fori_loop(0, blocks, query, 0)

    def hand_on_product(column_block, carry):
        hand_on(2, column_block)
        return carry

    lax.fori_loop(0, blocks, hand_on_product, 0)

    for array in range(3):

        def settle(column_block, carry):
            relay_copy(array, column_block).wait_send()
            for source_ref, owner in (
                (pack_ref.at[array, me_t, column_block], first_owner + column_block),
                (relay_ref.at[array, column_block], other_owner + column_block),
            ):

                @pl.when(owner == me_c)
                def _():
                    self_copy(array, source_ref).wait()

                @pl.when(owner != me_c)
                def _():
                    plane_copy(array, source_ref, owner, me_c).wait_send()
                    plane_copy(array, source_ref, owner, owner).wait_recv()

            return carry

        lax.fori_loop(0, blocks, settle, 0)


def out_kernel(
    ctx_count, tp_count,
    corr_ref, q_ref, k_ref, v_ref, out_grad_ref, taps_ref, skip_ref, tap_q_ref,
    before_ref, after_ref,
    grad_k_ref, grad_v_ref, total_ref,
    arrived, ext_q, ext_k, ext_v, grad_w, k_short, v_short, work, gk, gv, part, parts, summed,
    send_sem, recv_sem, self_sem, sum_send, sum_recv, spread_send, spread_recv,
):
    me_c, me_t = lax.axis_index("ctx"), lax.axis_index("tp")
    rows, width = q_ref.shape
    blocks = width // LANES
    half_rows = rows // 2
    more = half_rows + 8
    longer = rows + 8
    share = ctx_count // tp_count
    source_tp = me_c // share
    my_block = (me_c - source_tp * share) * tp_count + me_t
    meet_all(ctx_count, tp_count, me_c, me_t)

    def corr_rows(index):
        return corr_ref.at[pl.ds(pl.multiple_of(index * half_rows, half_rows), more)]

    def block_copy(index):
        return pltpu.make_async_remote_copy(
            src_ref=corr_rows(index),
            dst_ref=arrived.at[my_block],
            send_sem=send_sem.at[index],
            recv_sem=recv_sem.at[my_block],
            device_id={"ctx": index, "tp": source_tp},
            device_id_type=MESH,
        )

    def self_copy():
        return pltpu.make_async_copy(corr_rows(me_c), arrived.at[my_block], self_sem)

    def is_self(c, t):
        return jnp.logical_and(c == me_c, t == me_t)

    def launch(index, carry):
        mine = is_self(index, source_tp)

        @pl.when(mine)
        def _():
            self_copy().start()

        @pl.when(jnp.logical_not(mine))
        def _():
            block_copy(index).start()

        return carry

    lax.fori_loop(0, ctx_count, launch, 0)

    def prepare(column_block, carry):
        cols = column(column_block)
        extend(ext_q, q_ref, before_ref[0, :, cols], after_ref[0, :, cols], cols)
        extend(ext_k, k_ref, before_ref[1, :, cols], after_ref[1, :, cols], cols)
        extend(ext_v, v_ref, before_ref[2, :, cols], after_ref[2, :, cols], cols)
        q_short = short_filter(ext_q, taps_ref, 0, cols, longer)
        grad_w[0:rows, cols] = out_grad_ref[:, cols] * q_short[:rows]
        grad_w[rows:longer, cols] = after_ref[3, :, cols] * q_short[rows:]
        k_short[:, cols] = short_filter(ext_k, taps_ref, 1, cols, longer)
        v_short[:, cols] = short_filter(ext_v, taps_ref, 2, cols, longer)
        return carry

    lax.fori_loop(0, blocks, prepare, 0)

    def settle(index, carry):
        mine = is_self(index, source_tp)

        @pl.when(mine)
        def _():
            self_copy().wait()

        @pl.when(jnp.logical_not(mine))
        def _():
            block_copy(index).wait_send()

        owner_c, owner_t = me_t * share + index // tp_count, index % tp_count

        @pl.when(jnp.logical_not(is_self(owner_c, owner_t)))
        def _():
            pltpu.make_async_remote_copy(
                src_ref=corr_rows(index),
                dst_ref=arrived.at[index],
                send_sem=send_sem.at[index],
                recv_sem=recv_sem.at[index],
                device_id={"ctx": owner_c, "tp": owner_t},
                device_id_type=MESH,
            ).wait_recv()

        return carry

    lax.fori_loop(0, ctx_count, settle, 0)
    low = low_lanes((more, LANES))

    def finish(column_block, carry):
        cols = column(column_block)
        one, two = arrived[2 * column_block], arrived[2 * column_block + 1]
        work[pl.ds(0, more, stride=2), :] = jnp.where(low, one, swap(two))
        work[pl.ds(1, more, stride=2), :] = jnp.where(low, swap(one), two)
        extend(ext_k, k_ref, before_ref[1, :, cols], after_ref[1, :, cols], cols)
        extend(ext_v, v_ref, before_ref[2, :, cols], after_ref[2, :, cols], cols)
        weight, ks, vs = grad_w[:, cols], k_short[:, cols], v_short[:, cols]
        grad_z = skip_ref[0:1, cols] * weight + work[0:longer, :]
        gk[...] = grad_z * vs
        gv[...] = grad_z * ks
        grad_k_ref[:, cols] = long_gather(gk, taps_ref, 1, cols, rows)
        grad_v_ref[:, cols] = long_gather(gv, taps_ref, 2, cols, rows)
        sums = tap_rows(gk[0:rows, :], ext_k, rows) + tap_rows(gv[0:rows, :], ext_v, rows)
        skip = jnp.sum((weight * (ks * vs))[:rows], axis=0, keepdims=True)
        part[:, cols] = jnp.concatenate(
            [tap_q_ref[0:3, cols]] + sums + [skip, jnp.zeros((6, LANES), jnp.float32)], axis=0
        )
        return carry

    lax.fori_loop(0, blocks, finish, 0)

    def piece(ref, index):
        return ref.at[pl.ds(pl.multiple_of(index // blocks * 8, 8), 8), column(index % blocks)]

    def sum_copy(index, slot):
        return pltpu.make_async_remote_copy(
            src_ref=piece(part, index),
            dst_ref=parts.at[slot],
            send_sem=sum_send.at[index],
            recv_sem=sum_recv.at[slot],
            device_id={"ctx": index, "tp": me_t},
            device_id_type=MESH,
        )

    def spread_copy(index, slot):
        return pltpu.make_async_remote_copy(
            src_ref=summed,
            dst_ref=piece(total_ref, slot),
            send_sem=spread_send.at[index],
            recv_sem=spread_recv.at[slot],
            device_id={"ctx": index, "tp": me_t},
            device_id_type=MESH,
        )

    def others(action):
        def step(index, carry):
            @pl.when(index != me_c)
            def _():
                action(index)

            return carry

        lax.fori_loop(0, ctx_count, step, 0)

    others(lambda index: sum_copy(index, me_c).start())
    parts[me_c] = part[
        pl.ds(pl.multiple_of(me_c // blocks * 8, 8), 8), column(me_c % blocks)
    ]

    def sum_wait(index):
        sum_copy(index, me_c).wait_send()
        sum_copy(index, index).wait_recv()

    others(sum_wait)
    summed[...] = jnp.sum(parts[...], axis=0)
    others(lambda index: spread_copy(index, me_c).start())
    total_ref[pl.ds(pl.multiple_of(me_c // blocks * 8, 8), 8), column(me_c % blocks)] = summed[...]

    def spread_wait(index):
        spread_copy(index, me_c).wait_send()
        spread_copy(index, index).wait_recv()

    others(spread_wait)


def on_device(q_in, k_in, v_in, short_taps, long_filter, skip_gain, conv_saved, grad_out):
    rows, width = q_in.shape
    ctx_count, tp_count = lax.axis_size("ctx"), lax.axis_size("tp")
    group = width // ctx_count
    seq_total = rows * ctx_count
    fits = (
        tp_count == 2
        and group == HALF
        and ctx_count % 2 == 0
        and width == ctx_count // 2 * LANES
        and rows % 256 == 0
        and seq_total == 8192
    )
    if not fits:
        return on_device_general(
            q_in, k_in, v_in, short_taps, long_filter, skip_gain, conv_saved, grad_out
        )
    count = seq_total // 2
    f32 = jnp.float32
    vmem = pl.BlockSpec(memory_space=pltpu.VMEM)
    anywhere = pl.BlockSpec(memory_space=pl.ANY)
    shape = jax.ShapeDtypeStruct
    packed = shape((count, LANES), f32)
    dma = pltpu.SemaphoreType.DMA
    ext = pltpu.VMEM((rows + 16, LANES), f32)
    rf, rg, rk, grad_q, tap_q, before, after = pl.pallas_call(
        functools.partial(in_kernel, ctx_count, tp_count),
        out_shape=(
            packed, packed, packed,
            shape((rows, width), f32),
            shape((8, width), f32),
            shape((3, 8, width), f32),
            shape((5, 8, width), f32),
        ),
        in_specs=[vmem] * 7,
        out_specs=(anywhere, anywhere, anywhere, vmem, vmem, vmem, vmem),
        scratch_shapes=[
            pltpu.VMEM((3, 2, ctx_count // 2, rows // 2, LANES), f32),
            pltpu.VMEM((3, ctx_count // 2, rows // 2, LANES), f32),
            ext, ext, ext, ext, ext,
            dma((8,)), dma((8,)), dma((3, ctx_count)), dma((3, ctx_count)), dma((3,)),
            dma((3, ctx_count // 2)), dma((3, ctx_count // 2)),
        ],
        compiler_params=pltpu.CompilerParams(
            collective_id=0, has_side_effects=True, vmem_limit_bytes=56 * MIB
        ),
        name="send_in",
    )(q_in, k_in, v_in, short_taps, long_filter, conv_saved, grad_out)
    tables = [jnp.asarray(table) for table in dft_tables(seq_total)]
    corr, zeta = pl.pallas_call(
        fft_kernel,
        out_shape=(shape((count + 8, LANES), f32), packed),
        in_specs=[vmem] * 9,
        out_specs=(vmem, vmem),
        scratch_shapes=[
            pltpu.VMEM((2 * seq_total, LANES), f32),
            pltpu.VMEM((2 * seq_total, LANES), f32),
            pltpu.VMEM((2 * seq_total, LANES), f32),
        ],
        compiler_params=pltpu.CompilerParams(vmem_limit_bytes=60 * MIB),
        name="correlate",
    )(rf, rg, rk, *tables)
    longer = pltpu.VMEM((rows + 8, width), f32)
    grad_k, grad_v, total = pl.pallas_call(
        functools.partial(out_kernel, ctx_count, tp_count),
        out_shape=(shape((rows, width), f32), shape((rows, width), f32), shape((16, width), f32)),
        in_specs=[anywhere] + [vmem] * 9,
        out_specs=(vmem, vmem, vmem),
        scratch_shapes=[
            pltpu.VMEM((ctx_count, rows // 2 + 8, LANES), f32),
            ext, ext, ext, longer, longer, longer, ext,
            pltpu.VMEM((rows + 8, LANES), f32),
            pltpu.VMEM((rows + 8, LANES), f32),
            pltpu.VMEM((16, width), f32),
            pltpu.VMEM((ctx_count, 8, LANES), f32),
            pltpu.VMEM((8, LANES), f32),
            dma((ctx_count,)), dma((ctx_count,)), dma(()),
            dma((ctx_count,)), dma((ctx_count,)), dma((ctx_count,)), dma((ctx_count,)),
        ],
        compiler_params=pltpu.CompilerParams(
            collective_id=1, has_side_effects=True, vmem_limit_bytes=56 * MIB
        ),
        name="send_back",
    )(corr, q_in, k_in, v_in, grad_out, short_taps, skip_gain.reshape(1, width), tap_q, before, after)
    grad_filter = jnp.transpose(zeta.reshape(seq_total, HALF))
    return (grad_q, grad_k, grad_v, grad_filter, total[:9].reshape(3, 3, width), total[9])


def solution(mesh):
    placed = (
        P("ctx", "tp"),
        P("ctx", "tp"),
        P("ctx", "tp"),
        P(None, None, "tp"),
        P("ctx", "tp"),
        P("tp"),
        P("ctx", "tp"),
        P("ctx", "tp"),
    )
    return jax.shard_map(
        on_device,
        mesh=mesh,
        in_specs=placed,
        out_specs=(
            P("ctx", "tp"),
            P("ctx", "tp"),
            P("ctx", "tp"),
            P(("ctx", "tp"), None),
            P(None, None, "tp"),
            P("tp"),
        ),
        check_vma=False,
    )
```

```python
import functools
import math

import jax
import jax.numpy as jnp
import numpy as np
from jax import lax
from jax.experimental import pallas as pl
from jax.experimental.pallas import tpu as pltpu
from jax.sharding import PartitionSpec as P

highest = lax.Precision.HIGHEST


def passed_along(value, axis, steps):
    count = lax.axis_size(axis)
    leading, last = (max(0, -steps), min(count, count - steps))
    return lax.ppermute(value, axis, [(source, source + steps) for source in range(leading, last)])


def phase_table(index_product, modulus, direction):
    reduced = jnp.mod(index_product, modulus).astype(jnp.float32)
    radians = direction * 2.0 * math.pi / modulus * reduced
    return (jnp.cos(radians), jnp.sin(radians))


def complex_mul(left_real, left_imag, right_real, right_imag):
    return (
        left_real * right_real - left_imag * right_imag,
        left_real * right_imag + left_imag * right_real,
    )


def matmul_complex(form, table_cos, table_sin, data_real, data_imag):
    real_out = jnp.einsum(form, table_cos, data_real, precision=highest) - jnp.einsum(
        form, table_sin, data_imag, precision=highest
    )
    imag_out = jnp.einsum(form, table_cos, data_imag, precision=highest) + jnp.einsum(
        form, table_sin, data_real, precision=highest
    )
    return (real_out, imag_out)


def channel_correlate(filter_real, filter_imag, grad_w, ctx_count):
    local_rows = filter_real.shape[0]
    slab_width = filter_real.shape[1]
    group_width = slab_width // ctx_count
    seq_total = local_rows * ctx_count
    arrived = (
        lax.all_to_all(filter_real, "ctx", split_axis=1, concat_axis=0, tiled=True),
        lax.all_to_all(filter_imag, "ctx", split_axis=1, concat_axis=0, tiled=True),
        lax.all_to_all(grad_w, "ctx", split_axis=1, concat_axis=0, tiled=True),
    )
    block_shape = (ctx_count, local_rows, group_width)
    whole_real = arrived[0].reshape(block_shape)
    whole_imag = arrived[1].reshape(block_shape)
    whole_grad = arrived[2].reshape(block_shape)
    spectral_index = lax.iota(jnp.int32, 2 * ctx_count)
    device_index = lax.iota(jnp.int32, ctx_count)
    position = lax.iota(jnp.int32, local_rows)
    outer_cos, outer_sin = phase_table(
        spectral_index[:, None] * device_index[None, :], 2 * ctx_count, -1.0
    )
    filter_pair = matmul_complex("qd,djc->qjc", outer_cos, outer_sin, whole_real, whole_imag)
    grad_pair = (
        jnp.einsum("qd,djc->qjc", outer_cos, whole_grad, precision=highest),
        jnp.einsum("qd,djc->qjc", outer_sin, whole_grad, precision=highest),
    )
    twist_cos, twist_sin = phase_table(
        spectral_index[:, None] * position[None, :], 2 * seq_total, -1.0
    )
    filter_pair = complex_mul(
        filter_pair[0], filter_pair[1], twist_cos[:, :, None], twist_sin[:, :, None]
    )
    grad_pair = complex_mul(
        grad_pair[0], grad_pair[1], twist_cos[:, :, None], twist_sin[:, :, None]
    )
    inner_cos, inner_sin = phase_table(position[:, None] * position[None, :], local_rows, -1.0)
    filter_spec = matmul_complex(
        "jb,qjc->qbc", inner_cos, inner_sin, filter_pair[0], filter_pair[1]
    )
    grad_spec = matmul_complex("jb,qjc->qbc", inner_cos, inner_sin, grad_pair[0], grad_pair[1])
    product_real = filter_spec[0] * grad_spec[0] + filter_spec[1] * grad_spec[1]
    product_imag = filter_spec[0] * grad_spec[1] - filter_spec[1] * grad_spec[0]
    back_cos, back_sin = phase_table(position[:, None] * position[None, :], local_rows, 1.0)
    summed = matmul_complex("jb,qbc->qjc", back_cos, back_sin, product_real, product_imag)
    untwist_cos, untwist_sin = phase_table(
        spectral_index[:, None] * position[None, :], 2 * seq_total, 1.0
    )
    summed = complex_mul(summed[0], summed[1], untwist_cos[:, :, None], untwist_sin[:, :, None])
    final_cos, final_sin = phase_table(
        device_index[:, None] * spectral_index[None, :], 2 * ctx_count, 1.0
    )
    result = matmul_complex("dq,qjc->djc", final_cos, final_sin, summed[0], summed[1])
    factor = 1.0 / (2.0 * seq_total)
    flat_shape = (seq_total, group_width)
    returned = (
        lax.all_to_all(
            (result[0] * factor).reshape(flat_shape), "ctx", split_axis=0, concat_axis=1, tiled=True
        ),
        lax.all_to_all(
            (result[1] * factor).reshape(flat_shape), "ctx", split_axis=0, concat_axis=1, tiled=True
        ),
    )
    return (returned[0], returned[1])


def on_device_general(q_in, k_in, v_in, short_taps, long_filter, skip_gain, conv_saved, grad_out):
    local_rows = q_in.shape[0]
    slab_width = q_in.shape[1]
    ctx_count = lax.axis_size("ctx")
    tp_count = lax.axis_size("tp")
    seq_total = local_rows * ctx_count
    filter_scale = 1.0 / math.sqrt(seq_total)
    inputs = jnp.stack([q_in, k_in, v_in])
    previous = passed_along(inputs[:, local_rows - 2 :], "ctx", 1)
    extended = jnp.concatenate([previous, inputs], axis=1)
    first_tap = short_taps[:, 0][:, None, :]
    second_tap = short_taps[:, 1][:, None, :]
    third_tap = short_taps[:, 2][:, None, :]
    shorted = (
        first_tap * extended[:, 2:]
        + second_tap * extended[:, 1 : local_rows + 1]
        + third_tap * extended[:, :local_rows]
    )
    q_short = shorted[0]
    k_short = shorted[1]
    v_short = shorted[2]
    product_kv = k_short * v_short
    grad_w = grad_out * q_short
    grad_qs = grad_out * conv_saved
    corr_real, corr_imag = channel_correlate(long_filter, product_kv, grad_w, ctx_count)
    grad_z = skip_gain * grad_w + filter_scale * corr_real
    grad_long = -filter_scale * corr_imag
    grad_ks = grad_z * v_short
    grad_vs = grad_z * k_short
    grad_stack = jnp.stack([grad_qs, grad_ks, grad_vs])
    following = passed_along(grad_stack[:, :2], "ctx", -1)
    ext_grads = jnp.concatenate([grad_stack, following], axis=1)
    grad_inputs = (
        first_tap * ext_grads[:, :local_rows]
        + second_tap * ext_grads[:, 1 : local_rows + 1]
        + third_tap * ext_grads[:, 2:]
    )
    short_part = jnp.stack(
        [
            jnp.sum(grad_stack * extended[:, 2 - offset : 2 - offset + local_rows], axis=1)
            for offset in range(3)
        ],
        axis=1,
    )
    skip_part = jnp.sum(grad_w * product_kv, axis=0)
    short_total, skip_total = lax.psum((short_part, skip_part), "ctx")
    group_width = slab_width // ctx_count
    repeat = ctx_count // tp_count
    flipped = jnp.transpose(grad_long).reshape(repeat, tp_count * group_width, local_rows)
    settled = lax.all_to_all(
        lax.all_to_all(flipped, "tp", split_axis=1, concat_axis=0, tiled=True),
        "ctx",
        split_axis=0,
        concat_axis=2,
        tiled=True,
    )
    grad_filter = settled.reshape(group_width, seq_total)
    return (grad_inputs[0], grad_inputs[1], grad_inputs[2], grad_filter, short_total, skip_total)


MESH = pl.DeviceIdType.MESH
LANES = 128
HALF = 64
N2 = 128
MIB = 1 << 20


def split_table(table):
    high = table.astype(jnp.bfloat16)
    low = (table - high.astype(np.float64)).astype(jnp.bfloat16)
    return np.concatenate([high, high, low], axis=-1)


def split_data(data):
    high = data.astype(jnp.bfloat16)
    low = (data - high.astype(jnp.float32)).astype(jnp.bfloat16)
    return jnp.concatenate([high, low, high], axis=0)


def dft_tables(seq_total):
    n1_used = seq_total // 2 // N2
    n1_total = 2 * n1_used
    length = n1_total * N2
    n1 = np.arange(n1_used)
    k1 = np.arange(n1_total)
    n2 = np.arange(N2)
    turns = (n1[None, None, :] * k1[None, :, None] * N2 + n2[:, None, None] * k1[None, :, None]) % length
    angle = 2.0 * np.pi / length * turns
    cos, sin = np.cos(angle), np.sin(angle)
    first = np.concatenate(
        [np.concatenate([cos, sin], axis=2), np.concatenate([-sin, cos], axis=2)], axis=1
    )
    factor = 1.0 / (length * math.sqrt(seq_total))
    cos_t, sin_t = np.swapaxes(cos, 1, 2) * factor, np.swapaxes(sin, 1, 2) * factor
    last = np.concatenate(
        [np.concatenate([cos_t, -sin_t], axis=2), np.concatenate([-sin_t, -cos_t], axis=2)], axis=1
    )
    inner = 2.0 * np.pi / N2 * ((n2[:, None] * n2[None, :]) % N2)
    c, s = np.cos(inner), np.sin(inner)
    second = np.block([[c, s], [-s, c]])
    back = np.block([[c, -s], [s, c]])
    odd = (np.arange(LANES) >= HALF)[None, :]
    turn_k2 = (2.0 * np.pi / N2 * n2)[:, None]
    turn_k1 = (2.0 * np.pi / length * k1)[:, None]
    phase_k2 = np.concatenate(
        [np.where(odd, np.cos(turn_k2), 1.0), np.where(odd, np.sin(turn_k2), 0.0)], axis=0
    ).astype(np.float32)
    phase_k1 = np.stack(
        [np.where(odd, np.cos(turn_k1), 1.0), np.where(odd, np.sin(turn_k1), 0.0)], axis=1
    ).astype(np.float32)
    return (
        split_table(first),
        split_table(second),
        split_table(back),
        split_table(last),
        phase_k2,
        phase_k1,
    )


def low_lanes(shape):
    return lax.broadcasted_iota(jnp.int32, shape, 1) < HALF


def swap(value):
    return pltpu.roll(value, HALF, 1)


def fft_kernel(
    f_ref, g_ref, k_ref, first_ref, second_ref, back_ref, last_ref, phase2_ref, phase1_ref,
    corr_ref, filter_ref, yf_ref, yg_ref, z_ref, zeta_ref, turn_ref,
):
    n1_used = f_ref.shape[0] // N2
    n1_total = 2 * n1_used
    tail = corr_ref.shape[0] - f_ref.shape[0]
    corr_ref[pl.ds(f_ref.shape[0], tail), :] = jnp.zeros((tail, LANES), jnp.float32)

    def forward(n2, carry):
        rows = pl.ds(n2, n1_used, stride=N2)
        xg = g_ref[rows, :]
        left = jnp.concatenate([f_ref[rows, :], k_ref[rows, :]], axis=0)
        right = jnp.concatenate([xg, jnp.zeros_like(xg)], axis=0)
        data = jnp.concatenate([left, right], axis=1)
        out = jnp.dot(first_ref[n2], split_data(data), preferred_element_type=jnp.float32)
        for part in range(2):
            into = pl.ds(n2 + part * N2, n1_total, stride=2 * N2)
            piece = out[part * n1_total : (part + 1) * n1_total]
            yf_ref[into, :] = piece[:, :LANES]
            yg_ref[into, :] = piece[:, LANES:]
        return carry

    lax.fori_loop(0, N2, forward, 0, unroll=4)

    low = low_lanes((N2, LANES))

    def product(k1):
        rows = pl.ds(pl.multiple_of(k1 * 2 * N2, 2 * N2), 2 * N2)
        data = jnp.concatenate([yf_ref[rows, :], yg_ref[rows, :]], axis=1)
        out = jnp.dot(second_ref[...], split_data(data), preferred_element_type=jnp.float32)
        fr, fi = out[:N2, :LANES], out[N2:, :LANES]
        gr, gi = out[:N2, LANES:], out[N2:, LANES:]
        sfr, sfi, sgr, sgi = swap(fr), swap(fi), swap(gr), swap(gi)
        er, ei = jnp.where(low, fr, sfr), jnp.where(low, fi, sfi)
        our, oui = jnp.where(low, sfr, fr), jnp.where(low, sfi, fi)
        ar, ai = phase2_ref[:N2, :], phase2_ref[N2:, :]
        both = phase1_ref[k1]
        br, bi = both[0:1], both[1:2]
        tr = ar * br - ai * bi
        ti = ar * bi + ai * br
        hr = tr * sgr - ti * sgi
        hi = tr * sgi + ti * sgr
        pr = er * gr + ei * gi + our * hr + oui * hi
        pi = er * gi - ei * gr + our * hi - oui * hr
        return jnp.concatenate([pr, pi], axis=0)

    def middle(pair, carry):
        k1 = pair * 2
        data = jnp.concatenate([product(k1), product(k1 + 1)], axis=1)
        out = jnp.dot(back_ref[...], split_data(data), preferred_element_type=jnp.float32)
        for part in range(2):
            for which in range(2):
                into = pl.ds(part * n1_total + k1 + which, N2, stride=2 * n1_total)
                z_ref[into, :] = out[
                    part * N2 : (part + 1) * N2, which * LANES : (which + 1) * LANES
                ]
        return carry

    lax.fori_loop(0, n1_total // 2, middle, 0, unroll=2)

    def inverse(n2, carry):
        rows = pl.ds(pl.multiple_of(n2 * 2 * n1_total, 2 * n1_total), 2 * n1_total)
        out = jnp.dot(last_ref[n2], split_data(z_ref[rows, :]), preferred_element_type=jnp.float32)
        into = pl.ds(n2, n1_used, stride=N2)
        corr_ref[into, :] = out[:n1_used]
        zeta_ref[into, :] = out[n1_used:]
        return carry

    lax.fori_loop(0, N2, inverse, 0, unroll=4)

    lower = low_lanes((HALF, LANES))

    def turn(step, carry):
        start = pl.multiple_of(step * LANES, LANES)
        one, two = zeta_ref[pl.ds(start, HALF), :], zeta_ref[pl.ds(start + HALF, HALF), :]
        slot = step % 4
        turn_ref[slot, pl.ds(0, HALF, stride=2), :] = jnp.where(lower, one, swap(two))
        turn_ref[slot, pl.ds(1, HALF, stride=2), :] = jnp.where(lower, swap(one), two)
        turned = jnp.transpose(turn_ref[slot])
        filter_ref[:, pl.ds(2 * start, LANES)] = turned[:HALF]
        filter_ref[:, pl.ds(2 * start + LANES, LANES)] = turned[HALF:]
        return carry

    lax.fori_loop(0, zeta_ref.shape[0] // LANES, turn, 0, unroll=4)


def meet_all(ctx_count, tp_count, me_c, me_t):
    barrier = pltpu.get_barrier_semaphore()

    def greet(index, carry):
        c, t = index // tp_count, index % tp_count

        @pl.when(jnp.logical_or(c != me_c, t != me_t))
        def _():
            pl.semaphore_signal(barrier, inc=1, device_id={"ctx": c, "tp": t}, device_id_type=MESH)

        return carry

    lax.fori_loop(0, ctx_count * tp_count, greet, 0)
    pl.semaphore_wait(barrier, ctx_count * tp_count - 1)


def column(block):
    return pl.ds(pl.multiple_of(block * LANES, LANES), LANES)


def extend(ext_ref, array_ref, before, after, cols):
    rows = array_ref.shape[0]
    ext_ref[0:8, :] = before
    ext_ref[8 : 8 + rows, :] = array_ref[:, cols]
    ext_ref[8 + rows : 16 + rows, :] = after


def short_filter(ext_ref, taps_ref, branch, cols, count):
    return (
        taps_ref[branch, 0:1, cols] * ext_ref[8 : 8 + count, :]
        + taps_ref[branch, 1:2, cols] * ext_ref[7 : 7 + count, :]
        + taps_ref[branch, 2:3, cols] * ext_ref[6 : 6 + count, :]
    )


def long_gather(value_ref, taps_ref, branch, cols, count):
    return (
        taps_ref[branch, 0:1, cols] * value_ref[0:count, :]
        + taps_ref[branch, 1:2, cols] * value_ref[1 : 1 + count, :]
        + taps_ref[branch, 2:3, cols] * value_ref[2 : 2 + count, :]
    )


def tap_rows(value, ext_ref, count):
    return [
        jnp.sum(value * ext_ref[8 - o : 8 - o + count, :], axis=0, keepdims=True) for o in range(3)
    ]


def in_kernel(
    ctx_count, tp_count,
    q_ref, k_ref, v_ref, taps_ref, f_ref, saved_ref, out_grad_ref,
    rf_ref, rg_ref, rk_ref, grad_q_ref, tap_q_ref, before_ref, after_ref,
    pack_ref, relay_ref, ext_q, ext_k, ext_v, work, work2,
    halo_send, halo_recv, send_sem, recv_sem, self_sem, relay_send, relay_recv,
):
    me_c, me_t = lax.axis_index("ctx"), lax.axis_index("tp")
    rows, width = q_ref.shape
    blocks = width // LANES
    half_rows = rows // 2
    first_owner = me_t * (ctx_count // tp_count)
    other_owner = (1 - me_t) * (ctx_count // tp_count)
    received = (rf_ref, rg_ref, rk_ref)
    has_before, has_after = me_c > 0, me_c < ctx_count - 1
    low = low_lanes((half_rows, LANES))
    meet_all(ctx_count, tp_count, me_c, me_t)

    forward = [
        pltpu.make_async_remote_copy(
            src_ref=ref.at[pl.ds(rows - 8, 8)],
            dst_ref=before_ref.at[index],
            send_sem=halo_send.at[index],
            recv_sem=halo_recv.at[index],
            device_id={"ctx": jnp.minimum(me_c + 1, ctx_count - 1), "tp": me_t},
            device_id_type=MESH,
        )
        for index, ref in enumerate((q_ref, k_ref, v_ref))
    ]
    backward = [
        pltpu.make_async_remote_copy(
            src_ref=ref.at[pl.ds(0, 8)],
            dst_ref=after_ref.at[index],
            send_sem=halo_send.at[3 + index],
            recv_sem=halo_recv.at[3 + index],
            device_id={"ctx": jnp.maximum(me_c - 1, 0), "tp": me_t},
            device_id_type=MESH,
        )
        for index, ref in enumerate((q_ref, k_ref, v_ref, out_grad_ref, saved_ref))
    ]

    @pl.when(has_after)
    def _():
        for copy in forward:
            copy.start()

    @pl.when(has_before)
    def _():
        for copy in backward:
            copy.start()

    @pl.when(jnp.logical_not(has_before))
    def _():
        before_ref[...] = jnp.zeros_like(before_ref)

    @pl.when(jnp.logical_not(has_after))
    def _():
        after_ref[...] = jnp.zeros_like(after_ref)

    def landing(array, source):
        return received[array].at[pl.ds(pl.multiple_of(source * half_rows, half_rows), half_rows)]

    def plane_copy(array, source_ref, owner, source):
        return pltpu.make_async_remote_copy(
            src_ref=source_ref,
            dst_ref=landing(array, source),
            send_sem=send_sem.at[array, owner],
            recv_sem=recv_sem.at[array, source],
            device_id={"ctx": owner, "tp": me_t},
            device_id_type=MESH,
        )

    def self_copy(array, source_ref):
        return pltpu.make_async_copy(source_ref, landing(array, me_c), self_sem.at[array])

    def send_in_plane(array, source_ref, owner):
        @pl.when(owner == me_c)
        def _():
            self_copy(array, source_ref).start()

        @pl.when(owner != me_c)
        def _():
            plane_copy(array, source_ref, owner, me_c).start()

    def relay_copy(array, column_block):
        return pltpu.make_async_remote_copy(
            src_ref=pack_ref.at[array, 1 - me_t, column_block],
            dst_ref=relay_ref.at[array, column_block],
            send_sem=relay_send.at[array, column_block],
            recv_sem=relay_recv.at[array, column_block],
            device_id={"ctx": me_c, "tp": 1 - me_t},
            device_id_type=MESH,
        )

    def pack_and_send(array, column_block):
        even = work[pl.ds(0, half_rows, stride=2), :]
        odd = work[pl.ds(1, half_rows, stride=2), :]
        pack_ref[array, 0, column_block] = jnp.where(low, even, swap(odd))
        pack_ref[array, 1, column_block] = jnp.where(low, swap(even), odd)
        relay_copy(array, column_block).start()
        send_in_plane(array, pack_ref.at[array, me_t, column_block], first_owner + column_block)

    def hand_on(array, column_block):
        relay_copy(array, column_block).wait_recv()
        send_in_plane(array, relay_ref.at[array, column_block], other_owner + column_block)

    def send_filter(step, carry):
        column_block = (step + me_c) % blocks
        work[0:rows, :] = f_ref[:, column(column_block)]
        pack_and_send(0, column_block)
        return carry

    lax.fori_loop(0, blocks, send_filter, 0)

    @pl.when(has_after)
    def _():
        for copy in forward:
            copy.wait_send()
        for copy in backward:
            copy.wait_recv()

    @pl.when(has_before)
    def _():
        for copy in forward:
            copy.wait_recv()
        for copy in backward:
            copy.wait_send()

    def send_grad(step, carry):
        column_block = (step + me_c) % blocks
        cols = column(column_block)
        extend(ext_q, q_ref, before_ref[0, :, cols], after_ref[0, :, cols], cols)
        work[0:rows, :] = out_grad_ref[:, cols] * short_filter(ext_q, taps_ref, 0, cols, rows)
        pack_and_send(1, column_block)
        hand_on(0, column_block)
        return carry

    lax.fori_loop(0, blocks, send_grad, 0)

    def send_product(step, carry):
        column_block = (step + me_c) % blocks
        cols = column(column_block)
        extend(ext_k, k_ref, before_ref[1, :, cols], after_ref[1, :, cols], cols)
        extend(ext_v, v_ref, before_ref[2, :, cols], after_ref[2, :, cols], cols)
        work[0:rows, :] = short_filter(ext_k, taps_ref, 1, cols, rows) * short_filter(
            ext_v, taps_ref, 2, cols, rows
        )
        pack_and_send(2, column_block)
        hand_on(1, column_block)
        return carry

    lax.fori_loop(0, blocks, send_product, 0)

    def query(column_block, carry):
        cols = column(column_block)
        extend(ext_q, q_ref, before_ref[0, :, cols], after_ref[0, :, cols], cols)
        here = out_grad_ref[:, cols] * saved_ref[:, cols]
        work2[0:rows, :] = here
        work2[rows : rows + 8, :] = after_ref[3, :, cols] * after_ref[4, :, cols]
        grad_q_ref[:, cols] = long_gather(work2, taps_ref, 0, cols, rows)
        sums = tap_rows(here, ext_q, rows)
        tap_q_ref[:, cols] = jnp.concatenate(sums + [jnp.zeros((5, LANES), jnp.float32)], axis=0)
        return carry

    lax.fori_loop(0, blocks, query, 0)

    def hand_on_product(step, carry):
        column_block = (step + me_c) % blocks
        hand_on(2, column_block)
        return carry

    lax.fori_loop(0, blocks, hand_on_product, 0)

    for array in range(3):

        def settle(column_block, carry):
            relay_copy(array, column_block).wait_send()
            for source_ref, owner in (
                (pack_ref.at[array, me_t, column_block], first_owner + column_block),
                (relay_ref.at[array, column_block], other_owner + column_block),
            ):

                @pl.when(owner == me_c)
                def _():
                    self_copy(array, source_ref).wait()

                @pl.when(owner != me_c)
                def _():
                    plane_copy(array, source_ref, owner, me_c).wait_send()
                    plane_copy(array, source_ref, owner, owner).wait_recv()

            return carry

        lax.fori_loop(0, blocks, settle, 0)


def out_kernel(
    ctx_count, tp_count,
    corr_ref, q_ref, k_ref, v_ref, out_grad_ref, taps_ref, skip_ref, tap_q_ref,
    before_ref, after_ref,
    grad_k_ref, grad_v_ref, total_ref,
    arrived, ext_q, ext_k, ext_v, grad_w, k_short, v_short, work, gk, gv, part, parts, summed,
    send_sem, recv_sem, self_sem, sum_send, sum_recv, spread_send, spread_recv,
):
    me_c, me_t = lax.axis_index("ctx"), lax.axis_index("tp")
    rows, width = q_ref.shape
    blocks = width // LANES
    half_rows = rows // 2
    more = half_rows + 8
    longer = rows + 8
    share = ctx_count // tp_count
    source_tp = me_c // share
    my_block = (me_c - source_tp * share) * tp_count + me_t
    meet_all(ctx_count, tp_count, me_c, me_t)

    def corr_rows(index):
        return corr_ref.at[pl.ds(pl.multiple_of(index * half_rows, half_rows), more)]

    def block_copy(index):
        return pltpu.make_async_remote_copy(
            src_ref=corr_rows(index),
            dst_ref=arrived.at[my_block],
            send_sem=send_sem.at[index],
            recv_sem=recv_sem.at[my_block],
            device_id={"ctx": index, "tp": source_tp},
            device_id_type=MESH,
        )

    def self_copy():
        return pltpu.make_async_copy(corr_rows(me_c), arrived.at[my_block], self_sem)

    def is_self(c, t):
        return jnp.logical_and(c == me_c, t == me_t)

    def launch(step, carry):
        index = (me_c + step) % ctx_count
        mine = is_self(index, source_tp)

        @pl.when(mine)
        def _():
            self_copy().start()

        @pl.when(jnp.logical_not(mine))
        def _():
            block_copy(index).start()

        return carry

    lax.fori_loop(0, ctx_count, launch, 0)

    def prepare(column_block, carry):
        cols = column(column_block)
        extend(ext_q, q_ref, before_ref[0, :, cols], after_ref[0, :, cols], cols)
        extend(ext_k, k_ref, before_ref[1, :, cols], after_ref[1, :, cols], cols)
        extend(ext_v, v_ref, before_ref[2, :, cols], after_ref[2, :, cols], cols)
        q_short = short_filter(ext_q, taps_ref, 0, cols, longer)
        grad_w[0:rows, cols] = out_grad_ref[:, cols] * q_short[:rows]
        grad_w[rows:longer, cols] = after_ref[3, :, cols] * q_short[rows:]
        k_short[:, cols] = short_filter(ext_k, taps_ref, 1, cols, longer)
        v_short[:, cols] = short_filter(ext_v, taps_ref, 2, cols, longer)
        return carry

    lax.fori_loop(0, blocks, prepare, 0)

    @pl.when(source_tp == me_t)
    def _():
        self_copy().wait()

    low = low_lanes((more, LANES))

    def finish(step, carry):
        column_block = (me_c + blocks - step) % blocks
        cols = column(column_block)
        owner_c = me_t * share + column_block
        for owner_t in range(2):
            block = 2 * column_block + owner_t

            @pl.when(jnp.logical_not(is_self(owner_c, owner_t)))
            def _():
                pltpu.make_async_remote_copy(
                    src_ref=corr_rows(block),
                    dst_ref=arrived.at[block],
                    send_sem=send_sem.at[block],
                    recv_sem=recv_sem.at[block],
                    device_id={"ctx": owner_c, "tp": owner_t},
                    device_id_type=MESH,
                ).wait_recv()

        one, two = arrived[2 * column_block], arrived[2 * column_block + 1]
        work[pl.ds(0, more, stride=2), :] = jnp.where(low, one, swap(two))
        work[pl.ds(1, more, stride=2), :] = jnp.where(low, swap(one), two)
        extend(ext_k, k_ref, before_ref[1, :, cols], after_ref[1, :, cols], cols)
        extend(ext_v, v_ref, before_ref[2, :, cols], after_ref[2, :, cols], cols)
        weight, ks, vs = grad_w[:, cols], k_short[:, cols], v_short[:, cols]
        grad_z = skip_ref[0:1, cols] * weight + work[0:longer, :]
        gk[...] = grad_z * vs
        gv[...] = grad_z * ks
        grad_k_ref[:, cols] = long_gather(gk, taps_ref, 1, cols, rows)
        grad_v_ref[:, cols] = long_gather(gv, taps_ref, 2, cols, rows)
        sums = tap_rows(gk[0:rows, :], ext_k, rows) + tap_rows(gv[0:rows, :], ext_v, rows)
        skip = jnp.sum((weight * (ks * vs))[:rows], axis=0, keepdims=True)
        part[:, cols] = jnp.concatenate(
            [tap_q_ref[0:3, cols]] + sums + [skip, jnp.zeros((6, LANES), jnp.float32)], axis=0
        )
        return carry

    lax.fori_loop(0, blocks, finish, 0)

    def piece(ref, index):
        return ref.at[pl.ds(pl.multiple_of(index // blocks * 8, 8), 8), column(index % blocks)]

    def sum_copy(index, slot):
        return pltpu.make_async_remote_copy(
            src_ref=piece(part, index),
            dst_ref=parts.at[slot],
            send_sem=sum_send.at[index],
            recv_sem=sum_recv.at[slot],
            device_id={"ctx": index, "tp": me_t},
            device_id_type=MESH,
        )

    def spread_copy(index, slot):
        return pltpu.make_async_remote_copy(
            src_ref=summed,
            dst_ref=piece(total_ref, slot),
            send_sem=spread_send.at[index],
            recv_sem=spread_recv.at[slot],
            device_id={"ctx": index, "tp": me_t},
            device_id_type=MESH,
        )

    def others(action):
        def step(index, carry):
            @pl.when(index != me_c)
            def _():
                action(index)

            return carry

        lax.fori_loop(0, ctx_count, step, 0)

    others(lambda index: sum_copy(index, me_c).start())
    parts[me_c] = part[
        pl.ds(pl.multiple_of(me_c // blocks * 8, 8), 8), column(me_c % blocks)
    ]

    def sum_wait(index):
        sum_copy(index, me_c).wait_send()
        sum_copy(index, index).wait_recv()

    others(sum_wait)
    summed[...] = jnp.sum(parts[...], axis=0)
    others(lambda index: spread_copy(index, me_c).start())
    total_ref[pl.ds(pl.multiple_of(me_c // blocks * 8, 8), 8), column(me_c % blocks)] = summed[...]

    def spread_wait(index):
        spread_copy(index, me_c).wait_send()
        spread_copy(index, index).wait_recv()

    others(spread_wait)

    def settle(index, carry):
        @pl.when(jnp.logical_not(is_self(index, source_tp)))
        def _():
            block_copy(index).wait_send()

        return carry

    lax.fori_loop(0, ctx_count, settle, 0)


def on_device(q_in, k_in, v_in, short_taps, long_filter, skip_gain, conv_saved, grad_out):
    rows, width = q_in.shape
    ctx_count, tp_count = lax.axis_size("ctx"), lax.axis_size("tp")
    group = width // ctx_count
    seq_total = rows * ctx_count
    fits = (
        tp_count == 2
        and group == HALF
        and ctx_count % 2 == 0
        and width == ctx_count // 2 * LANES
        and rows % 256 == 0
        and seq_total == 8192
    )
    if not fits:
        return on_device_general(
            q_in, k_in, v_in, short_taps, long_filter, skip_gain, conv_saved, grad_out
        )
    count = seq_total // 2
    f32 = jnp.float32
    vmem = pl.BlockSpec(memory_space=pltpu.VMEM)
    anywhere = pl.BlockSpec(memory_space=pl.ANY)
    shape = jax.ShapeDtypeStruct
    packed = shape((count, LANES), f32)
    dma = pltpu.SemaphoreType.DMA
    ext = pltpu.VMEM((rows + 16, LANES), f32)
    rf, rg, rk, grad_q, tap_q, before, after = pl.pallas_call(
        functools.partial(in_kernel, ctx_count, tp_count),
        out_shape=(
            packed, packed, packed,
            shape((rows, width), f32),
            shape((8, width), f32),
            shape((3, 8, width), f32),
            shape((5, 8, width), f32),
        ),
        in_specs=[vmem] * 7,
        out_specs=(anywhere, anywhere, anywhere, vmem, vmem, vmem, vmem),
        scratch_shapes=[
            pltpu.VMEM((3, 2, ctx_count // 2, rows // 2, LANES), f32),
            pltpu.VMEM((3, ctx_count // 2, rows // 2, LANES), f32),
            ext, ext, ext, ext, ext,
            dma((8,)), dma((8,)), dma((3, ctx_count)), dma((3, ctx_count)), dma((3,)),
            dma((3, ctx_count // 2)), dma((3, ctx_count // 2)),
        ],
        compiler_params=pltpu.CompilerParams(
            collective_id=0, has_side_effects=True, vmem_limit_bytes=56 * MIB
        ),
        name="send_in",
    )(q_in, k_in, v_in, short_taps, long_filter, conv_saved, grad_out)
    tables = [jnp.asarray(table) for table in dft_tables(seq_total)]
    corr, grad_filter = pl.pallas_call(
        fft_kernel,
        out_shape=(shape((count + 8, LANES), f32), shape((HALF, seq_total), f32)),
        in_specs=[vmem] * 9,
        out_specs=(vmem, vmem),
        scratch_shapes=[
            pltpu.VMEM((2 * seq_total, LANES), f32),
            pltpu.VMEM((2 * seq_total, LANES), f32),
            pltpu.VMEM((2 * seq_total, LANES), f32),
            pltpu.VMEM((count, LANES), f32),
            pltpu.VMEM((4, LANES, LANES), f32),
        ],
        compiler_params=pltpu.CompilerParams(vmem_limit_bytes=60 * MIB),
        name="correlate",
    )(rf, rg, rk, *tables)
    longer = pltpu.VMEM((rows + 8, width), f32)
    grad_k, grad_v, total = pl.pallas_call(
        functools.partial(out_kernel, ctx_count, tp_count),
        out_shape=(shape((rows, width), f32), shape((rows, width), f32), shape((16, width), f32)),
        in_specs=[anywhere] + [vmem] * 9,
        out_specs=(vmem, vmem, vmem),
        scratch_shapes=[
            pltpu.VMEM((ctx_count, rows // 2 + 8, LANES), f32),
            ext, ext, ext, longer, longer, longer, ext,
            pltpu.VMEM((rows + 8, LANES), f32),
            pltpu.VMEM((rows + 8, LANES), f32),
            pltpu.VMEM((16, width), f32),
            pltpu.VMEM((ctx_count, 8, LANES), f32),
            pltpu.VMEM((8, LANES), f32),
            dma((ctx_count,)), dma((ctx_count,)), dma(()),
            dma((ctx_count,)), dma((ctx_count,)), dma((ctx_count,)), dma((ctx_count,)),
        ],
        compiler_params=pltpu.CompilerParams(
            collective_id=1, has_side_effects=True, vmem_limit_bytes=56 * MIB
        ),
        name="send_back",
    )(corr, q_in, k_in, v_in, grad_out, short_taps, skip_gain.reshape(1, width), tap_q, before, after)
    return (grad_q, grad_k, grad_v, grad_filter, total[:9].reshape(3, 3, width), total[9])


def solution(mesh):
    placed = (
        P("ctx", "tp"),
        P("ctx", "tp"),
        P("ctx", "tp"),
        P(None, None, "tp"),
        P("ctx", "tp"),
        P("tp"),
        P("ctx", "tp"),
        P("ctx", "tp"),
    )
    return jax.shard_map(
        on_device,
        mesh=mesh,
        in_specs=placed,
        out_specs=(
            P("ctx", "tp"),
            P("ctx", "tp"),
            P("ctx", "tp"),
            P(("ctx", "tp"), None),
            P(None, None, "tp"),
            P("tp"),
        ),
        check_vma=False,
    )
```

```python
import functools
import math

import jax
import jax.numpy as jnp
import numpy as np
from jax import lax
from jax.experimental import pallas as pl
from jax.experimental.pallas import tpu as pltpu
from jax.sharding import PartitionSpec as P

highest = lax.Precision.HIGHEST


def passed_along(value, axis, steps):
    count = lax.axis_size(axis)
    leading, last = (max(0, -steps), min(count, count - steps))
    return lax.ppermute(value, axis, [(source, source + steps) for source in range(leading, last)])


def phase_table(index_product, modulus, direction):
    reduced = jnp.mod(index_product, modulus).astype(jnp.float32)
    radians = direction * 2.0 * math.pi / modulus * reduced
    return (jnp.cos(radians), jnp.sin(radians))


def complex_mul(left_real, left_imag, right_real, right_imag):
    return (
        left_real * right_real - left_imag * right_imag,
        left_real * right_imag + left_imag * right_real,
    )


def matmul_complex(form, table_cos, table_sin, data_real, data_imag):
    real_out = jnp.einsum(form, table_cos, data_real, precision=highest) - jnp.einsum(
        form, table_sin, data_imag, precision=highest
    )
    imag_out = jnp.einsum(form, table_cos, data_imag, precision=highest) + jnp.einsum(
        form, table_sin, data_real, precision=highest
    )
    return (real_out, imag_out)


def channel_correlate(filter_real, filter_imag, grad_w, ctx_count):
    local_rows = filter_real.shape[0]
    slab_width = filter_real.shape[1]
    group_width = slab_width // ctx_count
    seq_total = local_rows * ctx_count
    arrived = (
        lax.all_to_all(filter_real, "ctx", split_axis=1, concat_axis=0, tiled=True),
        lax.all_to_all(filter_imag, "ctx", split_axis=1, concat_axis=0, tiled=True),
        lax.all_to_all(grad_w, "ctx", split_axis=1, concat_axis=0, tiled=True),
    )
    block_shape = (ctx_count, local_rows, group_width)
    whole_real = arrived[0].reshape(block_shape)
    whole_imag = arrived[1].reshape(block_shape)
    whole_grad = arrived[2].reshape(block_shape)
    spectral_index = lax.iota(jnp.int32, 2 * ctx_count)
    device_index = lax.iota(jnp.int32, ctx_count)
    position = lax.iota(jnp.int32, local_rows)
    outer_cos, outer_sin = phase_table(
        spectral_index[:, None] * device_index[None, :], 2 * ctx_count, -1.0
    )
    filter_pair = matmul_complex("qd,djc->qjc", outer_cos, outer_sin, whole_real, whole_imag)
    grad_pair = (
        jnp.einsum("qd,djc->qjc", outer_cos, whole_grad, precision=highest),
        jnp.einsum("qd,djc->qjc", outer_sin, whole_grad, precision=highest),
    )
    twist_cos, twist_sin = phase_table(
        spectral_index[:, None] * position[None, :], 2 * seq_total, -1.0
    )
    filter_pair = complex_mul(
        filter_pair[0], filter_pair[1], twist_cos[:, :, None], twist_sin[:, :, None]
    )
    grad_pair = complex_mul(
        grad_pair[0], grad_pair[1], twist_cos[:, :, None], twist_sin[:, :, None]
    )
    inner_cos, inner_sin = phase_table(position[:, None] * position[None, :], local_rows, -1.0)
    filter_spec = matmul_complex(
        "jb,qjc->qbc", inner_cos, inner_sin, filter_pair[0], filter_pair[1]
    )
    grad_spec = matmul_complex("jb,qjc->qbc", inner_cos, inner_sin, grad_pair[0], grad_pair[1])
    product_real = filter_spec[0] * grad_spec[0] + filter_spec[1] * grad_spec[1]
    product_imag = filter_spec[0] * grad_spec[1] - filter_spec[1] * grad_spec[0]
    back_cos, back_sin = phase_table(position[:, None] * position[None, :], local_rows, 1.0)
    summed = matmul_complex("jb,qbc->qjc", back_cos, back_sin, product_real, product_imag)
    untwist_cos, untwist_sin = phase_table(
        spectral_index[:, None] * position[None, :], 2 * seq_total, 1.0
    )
    summed = complex_mul(summed[0], summed[1], untwist_cos[:, :, None], untwist_sin[:, :, None])
    final_cos, final_sin = phase_table(
        device_index[:, None] * spectral_index[None, :], 2 * ctx_count, 1.0
    )
    result = matmul_complex("dq,qjc->djc", final_cos, final_sin, summed[0], summed[1])
    factor = 1.0 / (2.0 * seq_total)
    flat_shape = (seq_total, group_width)
    returned = (
        lax.all_to_all(
            (result[0] * factor).reshape(flat_shape), "ctx", split_axis=0, concat_axis=1, tiled=True
        ),
        lax.all_to_all(
            (result[1] * factor).reshape(flat_shape), "ctx", split_axis=0, concat_axis=1, tiled=True
        ),
    )
    return (returned[0], returned[1])


def on_device_general(q_in, k_in, v_in, short_taps, long_filter, skip_gain, conv_saved, grad_out):
    local_rows = q_in.shape[0]
    slab_width = q_in.shape[1]
    ctx_count = lax.axis_size("ctx")
    tp_count = lax.axis_size("tp")
    seq_total = local_rows * ctx_count
    filter_scale = 1.0 / math.sqrt(seq_total)
    inputs = jnp.stack([q_in, k_in, v_in])
    previous = passed_along(inputs[:, local_rows - 2 :], "ctx", 1)
    extended = jnp.concatenate([previous, inputs], axis=1)
    first_tap = short_taps[:, 0][:, None, :]
    second_tap = short_taps[:, 1][:, None, :]
    third_tap = short_taps[:, 2][:, None, :]
    shorted = (
        first_tap * extended[:, 2:]
        + second_tap * extended[:, 1 : local_rows + 1]
        + third_tap * extended[:, :local_rows]
    )
    q_short = shorted[0]
    k_short = shorted[1]
    v_short = shorted[2]
    product_kv = k_short * v_short
    grad_w = grad_out * q_short
    grad_qs = grad_out * conv_saved
    corr_real, corr_imag = channel_correlate(long_filter, product_kv, grad_w, ctx_count)
    grad_z = skip_gain * grad_w + filter_scale * corr_real
    grad_long = -filter_scale * corr_imag
    grad_ks = grad_z * v_short
    grad_vs = grad_z * k_short
    grad_stack = jnp.stack([grad_qs, grad_ks, grad_vs])
    following = passed_along(grad_stack[:, :2], "ctx", -1)
    ext_grads = jnp.concatenate([grad_stack, following], axis=1)
    grad_inputs = (
        first_tap * ext_grads[:, :local_rows]
        + second_tap * ext_grads[:, 1 : local_rows + 1]
        + third_tap * ext_grads[:, 2:]
    )
    short_part = jnp.stack(
        [
            jnp.sum(grad_stack * extended[:, 2 - offset : 2 - offset + local_rows], axis=1)
            for offset in range(3)
        ],
        axis=1,
    )
    skip_part = jnp.sum(grad_w * product_kv, axis=0)
    short_total, skip_total = lax.psum((short_part, skip_part), "ctx")
    group_width = slab_width // ctx_count
    repeat = ctx_count // tp_count
    flipped = jnp.transpose(grad_long).reshape(repeat, tp_count * group_width, local_rows)
    settled = lax.all_to_all(
        lax.all_to_all(flipped, "tp", split_axis=1, concat_axis=0, tiled=True),
        "ctx",
        split_axis=0,
        concat_axis=2,
        tiled=True,
    )
    grad_filter = settled.reshape(group_width, seq_total)
    return (grad_inputs[0], grad_inputs[1], grad_inputs[2], grad_filter, short_total, skip_total)


MESH = pl.DeviceIdType.MESH
LANES = 128
HALF = 64
N2 = 128
MIB = 1 << 20


def split_table(table):
    high = table.astype(jnp.bfloat16)
    low = (table - high.astype(np.float64)).astype(jnp.bfloat16)
    return np.concatenate([high, high, low], axis=-1)


def split_data(data):
    high = data.astype(jnp.bfloat16)
    low = (data - high.astype(jnp.float32)).astype(jnp.bfloat16)
    return jnp.concatenate([high, low, high], axis=0)


def dft_tables(seq_total):
    n1_used = seq_total // 2 // N2
    n1_total = 2 * n1_used
    length = n1_total * N2
    n1 = np.arange(n1_used)
    k1 = np.arange(n1_total)
    n2 = np.arange(N2)
    turns = (n1[None, None, :] * k1[None, :, None] * N2 + n2[:, None, None] * k1[None, :, None]) % length
    angle = 2.0 * np.pi / length * turns
    cos, sin = np.cos(angle), np.sin(angle)
    first = np.concatenate(
        [np.concatenate([cos, sin], axis=2), np.concatenate([-sin, cos], axis=2)], axis=1
    )
    factor = 1.0 / (length * math.sqrt(seq_total))
    cos_t, sin_t = np.swapaxes(cos, 1, 2) * factor, np.swapaxes(sin, 1, 2) * factor
    last = np.concatenate(
        [np.concatenate([cos_t, -sin_t], axis=2), np.concatenate([-sin_t, -cos_t], axis=2)], axis=1
    )
    inner = 2.0 * np.pi / N2 * ((n2[:, None] * n2[None, :]) % N2)
    c, s = np.cos(inner), np.sin(inner)
    second = np.block([[c, s], [-s, c]])
    back = np.block([[c, -s], [s, c]])
    odd = (np.arange(LANES) >= HALF)[None, :]
    turn_k2 = (2.0 * np.pi / N2 * n2)[:, None]
    turn_k1 = (2.0 * np.pi / length * k1)[:, None]
    phase_k2 = np.concatenate(
        [np.where(odd, np.cos(turn_k2), 1.0), np.where(odd, np.sin(turn_k2), 0.0)], axis=0
    ).astype(np.float32)
    phase_k1 = np.stack(
        [np.where(odd, np.cos(turn_k1), 1.0), np.where(odd, np.sin(turn_k1), 0.0)], axis=1
    ).astype(np.float32)
    return (
        split_table(first),
        split_table(second),
        split_table(back),
        split_table(last),
        phase_k2,
        phase_k1,
    )


def low_lanes(shape):
    return lax.broadcasted_iota(jnp.int32, shape, 1) < HALF


def swap(value):
    return pltpu.roll(value, HALF, 1)


def fft_kernel(
    f_ref, g_ref, k_ref, first_ref, second_ref, back_ref, last_ref, phase2_ref, phase1_ref,
    corr_ref, filter_ref, yf_ref, yg_ref, z_ref, zeta_ref, turn_ref,
):
    n1_used = f_ref.shape[0] // N2
    n1_total = 2 * n1_used
    tail = corr_ref.shape[0] - f_ref.shape[0]
    corr_ref[pl.ds(f_ref.shape[0], tail), :] = jnp.zeros((tail, LANES), jnp.float32)

    def forward(n2, carry):
        rows = pl.ds(n2, n1_used, stride=N2)
        xg = g_ref[rows, :]
        left = jnp.concatenate([f_ref[rows, :], k_ref[rows, :]], axis=0)
        right = jnp.concatenate([xg, jnp.zeros_like(xg)], axis=0)
        data = jnp.concatenate([left, right], axis=1)
        out = jnp.dot(first_ref[n2], split_data(data), preferred_element_type=jnp.float32)
        for part in range(2):
            into = pl.ds(n2 + part * N2, n1_total, stride=2 * N2)
            piece = out[part * n1_total : (part + 1) * n1_total]
            yf_ref[into, :] = piece[:, :LANES]
            yg_ref[into, :] = piece[:, LANES:]
        return carry

    lax.fori_loop(0, N2, forward, 0, unroll=8)

    low = low_lanes((N2, LANES))

    def product(k1):
        rows = pl.ds(pl.multiple_of(k1 * 2 * N2, 2 * N2), 2 * N2)
        data = jnp.concatenate([yf_ref[rows, :], yg_ref[rows, :]], axis=1)
        out = jnp.dot(second_ref[...], split_data(data), preferred_element_type=jnp.float32)
        fr, fi = out[:N2, :LANES], out[N2:, :LANES]
        gr, gi = out[:N2, LANES:], out[N2:, LANES:]
        sfr, sfi, sgr, sgi = swap(fr), swap(fi), swap(gr), swap(gi)
        er, ei = jnp.where(low, fr, sfr), jnp.where(low, fi, sfi)
        our, oui = jnp.where(low, sfr, fr), jnp.where(low, sfi, fi)
        ar, ai = phase2_ref[:N2, :], phase2_ref[N2:, :]
        both = phase1_ref[k1]
        br, bi = both[0:1], both[1:2]
        tr = ar * br - ai * bi
        ti = ar * bi + ai * br
        hr = tr * sgr - ti * sgi
        hi = tr * sgi + ti * sgr
        pr = er * gr + ei * gi + our * hr + oui * hi
        pi = er * gi - ei * gr + our * hi - oui * hr
        return jnp.concatenate([pr, pi], axis=0)

    def middle(pair, carry):
        k1 = pair * 2
        data = jnp.concatenate([product(k1), product(k1 + 1)], axis=1)
        out = jnp.dot(back_ref[...], split_data(data), preferred_element_type=jnp.float32)
        for part in range(2):
            for which in range(2):
                into = pl.ds(part * n1_total + k1 + which, N2, stride=2 * n1_total)
                z_ref[into, :] = out[
                    part * N2 : (part + 1) * N2, which * LANES : (which + 1) * LANES
                ]
        return carry

    lax.fori_loop(0, n1_total // 2, middle, 0, unroll=4)

    def inverse(n2, carry):
        rows = pl.ds(pl.multiple_of(n2 * 2 * n1_total, 2 * n1_total), 2 * n1_total)
        out = jnp.dot(last_ref[n2], split_data(z_ref[rows, :]), preferred_element_type=jnp.float32)
        into = pl.ds(n2, n1_used, stride=N2)
        corr_ref[into, :] = out[:n1_used]
        zeta_ref[into, :] = out[n1_used:]
        return carry

    lax.fori_loop(0, N2, inverse, 0, unroll=8)

    lower = low_lanes((HALF, LANES))

    def turn(step, carry):
        start = pl.multiple_of(step * LANES, LANES)
        one, two = zeta_ref[pl.ds(start, HALF), :], zeta_ref[pl.ds(start + HALF, HALF), :]
        slot = step % 4
        turn_ref[slot, pl.ds(0, HALF, stride=2), :] = jnp.where(lower, one, swap(two))
        turn_ref[slot, pl.ds(1, HALF, stride=2), :] = jnp.where(lower, swap(one), two)
        turned = jnp.transpose(turn_ref[slot])
        filter_ref[:, pl.ds(2 * start, LANES)] = turned[:HALF]
        filter_ref[:, pl.ds(2 * start + LANES, LANES)] = turned[HALF:]
        return carry

    lax.fori_loop(0, zeta_ref.shape[0] // LANES, turn, 0, unroll=4)


def meet_all(ctx_count, tp_count, me_c, me_t):
    barrier = pltpu.get_barrier_semaphore()

    def greet(index, carry):
        c, t = index // tp_count, index % tp_count

        @pl.when(jnp.logical_or(c != me_c, t != me_t))
        def _():
            pl.semaphore_signal(barrier, inc=1, device_id={"ctx": c, "tp": t}, device_id_type=MESH)

        return carry

    lax.fori_loop(0, ctx_count * tp_count, greet, 0)
    pl.semaphore_wait(barrier, ctx_count * tp_count - 1)


def column(block):
    return pl.ds(pl.multiple_of(block * LANES, LANES), LANES)


def extend(ext_ref, array_ref, before, after, cols):
    rows = array_ref.shape[0]
    ext_ref[0:8, :] = before
    ext_ref[8 : 8 + rows, :] = array_ref[:, cols]
    ext_ref[8 + rows : 16 + rows, :] = after


def short_filter(ext_ref, taps_ref, branch, cols, count):
    return (
        taps_ref[branch, 0:1, cols] * ext_ref[8 : 8 + count, :]
        + taps_ref[branch, 1:2, cols] * ext_ref[7 : 7 + count, :]
        + taps_ref[branch, 2:3, cols] * ext_ref[6 : 6 + count, :]
    )


def long_gather(value_ref, taps_ref, branch, cols, count):
    return (
        taps_ref[branch, 0:1, cols] * value_ref[0:count, :]
        + taps_ref[branch, 1:2, cols] * value_ref[1 : 1 + count, :]
        + taps_ref[branch, 2:3, cols] * value_ref[2 : 2 + count, :]
    )


def tap_rows(value, ext_ref, count):
    return [
        jnp.sum(value * ext_ref[8 - o : 8 - o + count, :], axis=0, keepdims=True) for o in range(3)
    ]


def in_kernel(
    ctx_count, tp_count,
    q_ref, k_ref, v_ref, taps_ref, f_ref, saved_ref, out_grad_ref,
    rf_ref, rg_ref, rk_ref, grad_q_ref, tap_q_ref, before_ref, after_ref,
    pack_ref, relay_ref, ext_q, ext_k, ext_v, work, work2,
    halo_send, halo_recv, send_sem, recv_sem, self_sem, relay_send, relay_recv,
):
    me_c, me_t = lax.axis_index("ctx"), lax.axis_index("tp")
    rows, width = q_ref.shape
    blocks = width // LANES
    half_rows = rows // 2
    first_owner = me_t * (ctx_count // tp_count)
    other_owner = (1 - me_t) * (ctx_count // tp_count)
    received = (rf_ref, rg_ref, rk_ref)
    has_before, has_after = me_c > 0, me_c < ctx_count - 1
    low = low_lanes((half_rows, LANES))
    meet_all(ctx_count, tp_count, me_c, me_t)

    forward = [
        pltpu.make_async_remote_copy(
            src_ref=ref.at[pl.ds(rows - 8, 8)],
            dst_ref=before_ref.at[index],
            send_sem=halo_send.at[index],
            recv_sem=halo_recv.at[index],
            device_id={"ctx": jnp.minimum(me_c + 1, ctx_count - 1), "tp": me_t},
            device_id_type=MESH,
        )
        for index, ref in enumerate((q_ref, k_ref, v_ref))
    ]
    backward = [
        pltpu.make_async_remote_copy(
            src_ref=ref.at[pl.ds(0, 8)],
            dst_ref=after_ref.at[index],
            send_sem=halo_send.at[3 + index],
            recv_sem=halo_recv.at[3 + index],
            device_id={"ctx": jnp.maximum(me_c - 1, 0), "tp": me_t},
            device_id_type=MESH,
        )
        for index, ref in enumerate((q_ref, k_ref, v_ref, out_grad_ref, saved_ref))
    ]

    @pl.when(has_after)
    def _():
        for copy in forward:
            copy.start()

    @pl.when(has_before)
    def _():
        for copy in backward:
            copy.start()

    @pl.when(jnp.logical_not(has_before))
    def _():
        before_ref[...] = jnp.zeros_like(before_ref)

    @pl.when(jnp.logical_not(has_after))
    def _():
        after_ref[...] = jnp.zeros_like(after_ref)

    def landing(array, source):
        return received[array].at[pl.ds(pl.multiple_of(source * half_rows, half_rows), half_rows)]

    def plane_copy(array, source_ref, owner, source):
        return pltpu.make_async_remote_copy(
            src_ref=source_ref,
            dst_ref=landing(array, source),
            send_sem=send_sem.at[array, owner],
            recv_sem=recv_sem.at[array, source],
            device_id={"ctx": owner, "tp": me_t},
            device_id_type=MESH,
        )

    def self_copy(array, source_ref):
        return pltpu.make_async_copy(source_ref, landing(array, me_c), self_sem.at[array])

    def send_in_plane(array, source_ref, owner):
        @pl.when(owner == me_c)
        def _():
            self_copy(array, source_ref).start()

        @pl.when(owner != me_c)
        def _():
            plane_copy(array, source_ref, owner, me_c).start()

    def relay_copy(array, column_block):
        return pltpu.make_async_remote_copy(
            src_ref=pack_ref.at[array, 1 - me_t, column_block],
            dst_ref=relay_ref.at[array, column_block],
            send_sem=relay_send.at[array, column_block],
            recv_sem=relay_recv.at[array, column_block],
            device_id={"ctx": me_c, "tp": 1 - me_t},
            device_id_type=MESH,
        )

    def pack_and_send(array, column_block):
        even = work[pl.ds(0, half_rows, stride=2), :]
        odd = work[pl.ds(1, half_rows, stride=2), :]
        pack_ref[array, 0, column_block] = jnp.where(low, even, swap(odd))
        pack_ref[array, 1, column_block] = jnp.where(low, swap(even), odd)
        relay_copy(array, column_block).start()
        send_in_plane(array, pack_ref.at[array, me_t, column_block], first_owner + column_block)

    def hand_on(array, column_block):
        relay_copy(array, column_block).wait_recv()
        send_in_plane(array, relay_ref.at[array, column_block], other_owner + column_block)

    def send_filter(step, carry):
        column_block = (step + me_c) % blocks
        work[0:rows, :] = f_ref[:, column(column_block)]
        pack_and_send(0, column_block)
        return carry

    lax.fori_loop(0, blocks, send_filter, 0)

    @pl.when(has_after)
    def _():
        for copy in forward:
            copy.wait_send()
        for copy in backward:
            copy.wait_recv()

    @pl.when(has_before)
    def _():
        for copy in forward:
            copy.wait_recv()
        for copy in backward:
            copy.wait_send()

    def send_grad(step, carry):
        column_block = (step + me_c) % blocks
        cols = column(column_block)
        extend(ext_q, q_ref, before_ref[0, :, cols], after_ref[0, :, cols], cols)
        work[0:rows, :] = out_grad_ref[:, cols] * short_filter(ext_q, taps_ref, 0, cols, rows)
        pack_and_send(1, column_block)
        hand_on(0, column_block)
        return carry

    lax.fori_loop(0, blocks, send_grad, 0)

    def send_product(step, carry):
        column_block = (step + me_c) % blocks
        cols = column(column_block)
        extend(ext_k, k_ref, before_ref[1, :, cols], after_ref[1, :, cols], cols)
        extend(ext_v, v_ref, before_ref[2, :, cols], after_ref[2, :, cols], cols)
        work[0:rows, :] = short_filter(ext_k, taps_ref, 1, cols, rows) * short_filter(
            ext_v, taps_ref, 2, cols, rows
        )
        pack_and_send(2, column_block)
        hand_on(1, column_block)
        return carry

    lax.fori_loop(0, blocks, send_product, 0)

    def query(column_block, carry):
        cols = column(column_block)
        extend(ext_q, q_ref, before_ref[0, :, cols], after_ref[0, :, cols], cols)
        here = out_grad_ref[:, cols] * saved_ref[:, cols]
        work2[0:rows, :] = here
        work2[rows : rows + 8, :] = after_ref[3, :, cols] * after_ref[4, :, cols]
        grad_q_ref[:, cols] = long_gather(work2, taps_ref, 0, cols, rows)
        sums = tap_rows(here, ext_q, rows)
        tap_q_ref[:, cols] = jnp.concatenate(sums + [jnp.zeros((5, LANES), jnp.float32)], axis=0)
        return carry

    lax.fori_loop(0, blocks, query, 0)

    def hand_on_product(step, carry):
        column_block = (step + me_c) % blocks
        hand_on(2, column_block)
        return carry

    lax.fori_loop(0, blocks, hand_on_product, 0)

    for array in range(3):

        def settle(column_block, carry):
            relay_copy(array, column_block).wait_send()
            for source_ref, owner in (
                (pack_ref.at[array, me_t, column_block], first_owner + column_block),
                (relay_ref.at[array, column_block], other_owner + column_block),
            ):

                @pl.when(owner == me_c)
                def _():
                    self_copy(array, source_ref).wait()

                @pl.when(owner != me_c)
                def _():
                    plane_copy(array, source_ref, owner, me_c).wait_send()
                    plane_copy(array, source_ref, owner, owner).wait_recv()

            return carry

        lax.fori_loop(0, blocks, settle, 0)


def out_kernel(
    ctx_count, tp_count,
    corr_ref, q_ref, k_ref, v_ref, out_grad_ref, taps_ref, skip_ref, tap_q_ref,
    before_ref, after_ref,
    grad_k_ref, grad_v_ref, total_ref,
    arrived, ext_q, ext_k, ext_v, grad_w, k_short, v_short, work, gk, gv, part, parts, summed,
    send_sem, recv_sem, self_sem, sum_send, sum_recv, spread_send, spread_recv,
):
    me_c, me_t = lax.axis_index("ctx"), lax.axis_index("tp")
    rows, width = q_ref.shape
    blocks = width // LANES
    half_rows = rows // 2
    more = half_rows + 8
    longer = rows + 8
    share = ctx_count // tp_count
    source_tp = me_c // share
    my_block = (me_c - source_tp * share) * tp_count + me_t
    meet_all(ctx_count, tp_count, me_c, me_t)

    def corr_rows(index):
        return corr_ref.at[pl.ds(pl.multiple_of(index * half_rows, half_rows), more)]

    def block_copy(index):
        return pltpu.make_async_remote_copy(
            src_ref=corr_rows(index),
            dst_ref=arrived.at[my_block],
            send_sem=send_sem.at[index],
            recv_sem=recv_sem.at[my_block],
            device_id={"ctx": index, "tp": source_tp},
            device_id_type=MESH,
        )

    def self_copy():
        return pltpu.make_async_copy(corr_rows(me_c), arrived.at[my_block], self_sem)

    def is_self(c, t):
        return jnp.logical_and(c == me_c, t == me_t)

    def launch(step, carry):
        index = (me_c + ctx_count // 2 + step) % ctx_count
        mine = is_self(index, source_tp)

        @pl.when(mine)
        def _():
            self_copy().start()

        @pl.when(jnp.logical_not(mine))
        def _():
            block_copy(index).start()

        return carry

    lax.fori_loop(0, ctx_count, launch, 0)

    def prepare(column_block, carry):
        cols = column(column_block)
        extend(ext_q, q_ref, before_ref[0, :, cols], after_ref[0, :, cols], cols)
        extend(ext_k, k_ref, before_ref[1, :, cols], after_ref[1, :, cols], cols)
        extend(ext_v, v_ref, before_ref[2, :, cols], after_ref[2, :, cols], cols)
        q_short = short_filter(ext_q, taps_ref, 0, cols, longer)
        grad_w[0:rows, cols] = out_grad_ref[:, cols] * q_short[:rows]
        grad_w[rows:longer, cols] = after_ref[3, :, cols] * q_short[rows:]
        k_short[:, cols] = short_filter(ext_k, taps_ref, 1, cols, longer)
        v_short[:, cols] = short_filter(ext_v, taps_ref, 2, cols, longer)
        return carry

    lax.fori_loop(0, blocks, prepare, 0)

    @pl.when(source_tp == me_t)
    def _():
        self_copy().wait()

    low = low_lanes((more, LANES))

    def finish(step, carry):
        column_block = (me_c + blocks - step) % blocks
        cols = column(column_block)
        owner_c = me_t * share + column_block
        for owner_t in range(2):
            block = 2 * column_block + owner_t

            @pl.when(jnp.logical_not(is_self(owner_c, owner_t)))
            def _():
                pltpu.make_async_remote_copy(
                    src_ref=corr_rows(block),
                    dst_ref=arrived.at[block],
                    send_sem=send_sem.at[block],
                    recv_sem=recv_sem.at[block],
                    device_id={"ctx": owner_c, "tp": owner_t},
                    device_id_type=MESH,
                ).wait_recv()

        one, two = arrived[2 * column_block], arrived[2 * column_block + 1]
        work[pl.ds(0, more, stride=2), :] = jnp.where(low, one, swap(two))
        work[pl.ds(1, more, stride=2), :] = jnp.where(low, swap(one), two)
        extend(ext_k, k_ref, before_ref[1, :, cols], after_ref[1, :, cols], cols)
        extend(ext_v, v_ref, before_ref[2, :, cols], after_ref[2, :, cols], cols)
        weight, ks, vs = grad_w[:, cols], k_short[:, cols], v_short[:, cols]
        grad_z = skip_ref[0:1, cols] * weight + work[0:longer, :]
        gk[...] = grad_z * vs
        gv[...] = grad_z * ks
        grad_k_ref[:, cols] = long_gather(gk, taps_ref, 1, cols, rows)
        grad_v_ref[:, cols] = long_gather(gv, taps_ref, 2, cols, rows)
        sums = tap_rows(gk[0:rows, :], ext_k, rows) + tap_rows(gv[0:rows, :], ext_v, rows)
        skip = jnp.sum((weight * (ks * vs))[:rows], axis=0, keepdims=True)
        part[:, cols] = jnp.concatenate(
            [tap_q_ref[0:3, cols]] + sums + [skip, jnp.zeros((6, LANES), jnp.float32)], axis=0
        )
        return carry

    lax.fori_loop(0, blocks, finish, 0)

    def piece(ref, index):
        return ref.at[pl.ds(pl.multiple_of(index // blocks * 8, 8), 8), column(index % blocks)]

    def sum_copy(index, slot):
        return pltpu.make_async_remote_copy(
            src_ref=piece(part, index),
            dst_ref=parts.at[slot],
            send_sem=sum_send.at[index],
            recv_sem=sum_recv.at[slot],
            device_id={"ctx": index, "tp": me_t},
            device_id_type=MESH,
        )

    def spread_copy(index, slot):
        return pltpu.make_async_remote_copy(
            src_ref=summed,
            dst_ref=piece(total_ref, slot),
            send_sem=spread_send.at[index],
            recv_sem=spread_recv.at[slot],
            device_id={"ctx": index, "tp": me_t},
            device_id_type=MESH,
        )

    def others(action):
        def step(index, carry):
            @pl.when(index != me_c)
            def _():
                action(index)

            return carry

        lax.fori_loop(0, ctx_count, step, 0)

    others(lambda index: sum_copy(index, me_c).start())
    parts[me_c] = part[
        pl.ds(pl.multiple_of(me_c // blocks * 8, 8), 8), column(me_c % blocks)
    ]

    def sum_wait(index):
        sum_copy(index, me_c).wait_send()
        sum_copy(index, index).wait_recv()

    others(sum_wait)
    summed[...] = jnp.sum(parts[...], axis=0)
    others(lambda index: spread_copy(index, me_c).start())
    total_ref[pl.ds(pl.multiple_of(me_c // blocks * 8, 8), 8), column(me_c % blocks)] = summed[...]

    def spread_wait(index):
        spread_copy(index, me_c).wait_send()
        spread_copy(index, index).wait_recv()

    others(spread_wait)

    def settle(index, carry):
        @pl.when(jnp.logical_not(is_self(index, source_tp)))
        def _():
            block_copy(index).wait_send()

        return carry

    lax.fori_loop(0, ctx_count, settle, 0)


def on_device(q_in, k_in, v_in, short_taps, long_filter, skip_gain, conv_saved, grad_out):
    rows, width = q_in.shape
    ctx_count, tp_count = lax.axis_size("ctx"), lax.axis_size("tp")
    group = width // ctx_count
    seq_total = rows * ctx_count
    fits = (
        tp_count == 2
        and group == HALF
        and ctx_count % 2 == 0
        and width == ctx_count // 2 * LANES
        and rows % 256 == 0
        and seq_total == 8192
    )
    if not fits:
        return on_device_general(
            q_in, k_in, v_in, short_taps, long_filter, skip_gain, conv_saved, grad_out
        )
    count = seq_total // 2
    f32 = jnp.float32
    vmem = pl.BlockSpec(memory_space=pltpu.VMEM)
    anywhere = pl.BlockSpec(memory_space=pl.ANY)
    shape = jax.ShapeDtypeStruct
    packed = shape((count, LANES), f32)
    dma = pltpu.SemaphoreType.DMA
    ext = pltpu.VMEM((rows + 16, LANES), f32)
    rf, rg, rk, grad_q, tap_q, before, after = pl.pallas_call(
        functools.partial(in_kernel, ctx_count, tp_count),
        out_shape=(
            packed, packed, packed,
            shape((rows, width), f32),
            shape((8, width), f32),
            shape((3, 8, width), f32),
            shape((5, 8, width), f32),
        ),
        in_specs=[vmem] * 7,
        out_specs=(anywhere, anywhere, anywhere, vmem, vmem, vmem, vmem),
        scratch_shapes=[
            pltpu.VMEM((3, 2, ctx_count // 2, rows // 2, LANES), f32),
            pltpu.VMEM((3, ctx_count // 2, rows // 2, LANES), f32),
            ext, ext, ext, ext, ext,
            dma((8,)), dma((8,)), dma((3, ctx_count)), dma((3, ctx_count)), dma((3,)),
            dma((3, ctx_count // 2)), dma((3, ctx_count // 2)),
        ],
        compiler_params=pltpu.CompilerParams(
            collective_id=0, has_side_effects=True, vmem_limit_bytes=56 * MIB
        ),
        name="send_in",
    )(q_in, k_in, v_in, short_taps, long_filter, conv_saved, grad_out)
    tables = [jnp.asarray(table) for table in dft_tables(seq_total)]
    corr, grad_filter = pl.pallas_call(
        fft_kernel,
        out_shape=(shape((count + 8, LANES), f32), shape((HALF, seq_total), f32)),
        in_specs=[vmem] * 9,
        out_specs=(vmem, vmem),
        scratch_shapes=[
            pltpu.VMEM((2 * seq_total, LANES), f32),
            pltpu.VMEM((2 * seq_total, LANES), f32),
            pltpu.VMEM((2 * seq_total, LANES), f32),
            pltpu.VMEM((count, LANES), f32),
            pltpu.VMEM((4, LANES, LANES), f32),
        ],
        compiler_params=pltpu.CompilerParams(vmem_limit_bytes=60 * MIB),
        name="correlate",
    )(rf, rg, rk, *tables)
    longer = pltpu.VMEM((rows + 8, width), f32)
    grad_k, grad_v, total = pl.pallas_call(
        functools.partial(out_kernel, ctx_count, tp_count),
        out_shape=(shape((rows, width), f32), shape((rows, width), f32), shape((16, width), f32)),
        in_specs=[anywhere] + [vmem] * 9,
        out_specs=(vmem, vmem, vmem),
        scratch_shapes=[
            pltpu.VMEM((ctx_count, rows // 2 + 8, LANES), f32),
            ext, ext, ext, longer, longer, longer, ext,
            pltpu.VMEM((rows + 8, LANES), f32),
            pltpu.VMEM((rows + 8, LANES), f32),
            pltpu.VMEM((16, width), f32),
            pltpu.VMEM((ctx_count, 8, LANES), f32),
            pltpu.VMEM((8, LANES), f32),
            dma((ctx_count,)), dma((ctx_count,)), dma(()),
            dma((ctx_count,)), dma((ctx_count,)), dma((ctx_count,)), dma((ctx_count,)),
        ],
        compiler_params=pltpu.CompilerParams(
            collective_id=1, has_side_effects=True, vmem_limit_bytes=56 * MIB
        ),
        name="send_back",
    )(corr, q_in, k_in, v_in, grad_out, short_taps, skip_gain.reshape(1, width), tap_q, before, after)
    return (grad_q, grad_k, grad_v, grad_filter, total[:9].reshape(3, 3, width), total[9])


def solution(mesh):
    placed = (
        P("ctx", "tp"),
        P("ctx", "tp"),
        P("ctx", "tp"),
        P(None, None, "tp"),
        P("ctx", "tp"),
        P("tp"),
        P("ctx", "tp"),
        P("ctx", "tp"),
    )
    return jax.shard_map(
        on_device,
        mesh=mesh,
        in_specs=placed,
        out_specs=(
            P("ctx", "tp"),
            P("ctx", "tp"),
            P("ctx", "tp"),
            P(("ctx", "tp"), None),
            P(None, None, "tp"),
            P("tp"),
        ),
        check_vma=False,
    )
```
